512 devices in a mesh: nodes: 256 (over z, y, x), heads: 2 (over core).
Axes of the slice: x: 4, y: 8, z: 8, core: 2. Of those that a mesh axis runs over, the one named last changes fastest.
Arguments:
- grid_fields: bfloat16 [100, 131072], P(None, ('nodes', 'heads')), may hold values from -6 to 6
- mesh_state: bfloat16 [32768, 1024], P('nodes'), may hold values from -6 to 6
- w_embed: bfloat16 [100, 1024], replicated, may hold values from -0.625 to 0.625
- w_query_enc: bfloat16 [1024, 1024], P(None, 'heads'), may hold values from -0.1875 to 0.1875
- w_key_enc: bfloat16 [1024, 1024], P(None, 'heads'), may hold values from -0.1875 to 0.1875
- w_value_enc: bfloat16 [1024, 1024], P(None, 'heads'), may hold values from -0.1875 to 0.1875
- w_out_enc: bfloat16 [1024, 1024], P('heads'), may hold values from -0.1875 to 0.1875
- w_query_proc: bfloat16 [1024, 1024], P(None, 'heads'), may hold values from -0.1875 to 0.1875
- w_key_proc: bfloat16 [1024, 1024], P(None, 'heads'), may hold values from -0.1875 to 0.1875
- w_value_proc: bfloat16 [1024, 1024], P(None, 'heads'), may hold values from -0.1875 to 0.1875
- w_out_proc: bfloat16 [1024, 1024], P('heads'), may hold values from -0.1875 to 0.1875
- send_rows: int32 [256, 4, 32], P('nodes'), may hold values from 0 to 511
- edge_senders: int32 [32768, 32], P('nodes'), may hold values from 0 to 639, as said below
- edge_mask: int32 [32768, 32], P('nodes'), may hold values from 0 to 1, as said below
Outputs:
- layer_out: bfloat16 [32768, 1024], P(('nodes', 'heads'))
The draws below stay inside these ranges and needn't reach their ends.
Inputs may be any that keep to these rules, and one draw needn't show every extreme that they name: `edge_senders`: about three quarters of the edge slots point into the own region's rows, the rest into the neighbours' listed rows. `edge_mask`: the live edge slots of each mesh node come first, and every mesh node has at least one.
All inputs are finite; a program needn't handle non-finite values.
Results may differ from the reference program's by a relative error of at most 0.012.
Values may be sent and summed in bfloat16 or wider, within the bound.
A program may use at most 128 MiB of HBM per device.

```python
import math
import jax
import jax.numpy as jnp
from jax import lax

CH = 100
MODEL_WIDTH = 1024
HEADS = 16
HS = 64
FAN = 32
NEIGH = 4
GRID_REG = 512
REGION_MESH_NODES = 128
CAP = 32
GROUPS = 256
GRID_POINTS = 131072
MESH_NODES = 32768


def draw_edge_mask(key, part):
    key = jax.random.fold_in(key, 7)
    top_key, count_key = jax.random.split(key)
    region_top = jax.random.randint(top_key, (GROUPS,), FAN // 2, FAN + 1)
    node_top = jnp.repeat(region_top, REGION_MESH_NODES)
    spread = jax.random.randint(count_key, (MESH_NODES,), 0, 65536)
    counts = node_top - spread % ((node_top + 1) // 2)
    positions = jnp.arange(FAN, dtype=jnp.int32)
    return (positions[None, :] < counts[:, None]).astype(jnp.int32)


def draw_edge_senders(key, part):
    key = jax.random.fold_in(key, 11)
    pick_key, local_key, remote_key = jax.random.split(key, 3)
    pick = jax.random.randint(pick_key, (MESH_NODES, FAN), 0, 4)
    local_rows = jax.random.randint(local_key, (MESH_NODES, FAN), 0, GRID_REG)
    remote_rows = GRID_REG + jax.random.randint(remote_key, (MESH_NODES, FAN), 0, NEIGH * CAP)
    rows = jnp.where(pick == 0, remote_rows, local_rows).astype(jnp.int32)
    rows = rows.at[0, 0].set(GRID_REG + NEIGH * CAP - 1)
    return rows.at[1, 0].set(0)


def plant(values, key, smallest, high):
    dims = values.shape
    index_at = [jax.random.randint(jax.random.fold_in(key, axis), (), 0, dims[axis]) for axis in range(len(dims))]
    values = values.at[tuple(index_at)].set(smallest)
    longest = dims.index(max(dims))
    index_at[longest] = (index_at[longest] + 1) % dims[longest]
    return values.at[tuple(index_at)].set(high)


def block_scale(key, dims, shards, least, high):
    gain = 1.0
    for position, shards_of in shards:
        steps = jax.random.uniform(jax.random.fold_in(jax.random.fold_in(key, 6), position), (shards_of,), jnp.float32, least / len(shards), high / len(shards))
        gain = gain * jnp.repeat(jnp.exp(steps), dims[position] // shards_of).reshape((-1,) + (1,) * (len(dims) - 1 - position))
    return gain


def bell_draw(own_key, extent, scale, limit, pieces=(), held_as=jnp.bfloat16):
    level = block_scale(own_key, extent, pieces, -0.22, 0.18) if pieces else 1.0
    values = jax.random.normal(own_key, extent, jnp.float32) * scale * level
    return jnp.minimum(jnp.maximum(values, -limit), limit).astype(held_as)


def setup_inputs(seed: int = 0) -> dict:
    key_of = jax.random.split(jax.random.key(seed), 15)
    grid_fields = bell_draw(key_of[0], (CH, GRID_POINTS), 1.0, 6.0, ((1, 512),))
    mesh_state = bell_draw(key_of[1], (MESH_NODES, MODEL_WIDTH), 1.0, 6.0, ((0, 256),))
    w_embed = bell_draw(key_of[2], (CH, MODEL_WIDTH), CH ** -0.5, 0.625)
    w_query_enc = bell_draw(key_of[3], (MODEL_WIDTH, MODEL_WIDTH), MODEL_WIDTH ** -0.5, 0.1875, ((1, 2),))
    w_key_enc = bell_draw(key_of[4], (MODEL_WIDTH, MODEL_WIDTH), MODEL_WIDTH ** -0.5, 0.1875, ((1, 2),))
    w_value_enc = bell_draw(key_of[5], (MODEL_WIDTH, MODEL_WIDTH), MODEL_WIDTH ** -0.5, 0.1875, ((1, 2),))
    w_out_enc = bell_draw(key_of[6], (MODEL_WIDTH, MODEL_WIDTH), MODEL_WIDTH ** -0.5, 0.1875, ((0, 2),))
    w_query_proc = bell_draw(key_of[7], (MODEL_WIDTH, MODEL_WIDTH), MODEL_WIDTH ** -0.5, 0.1875, ((1, 2),))
    w_key_proc = bell_draw(key_of[8], (MODEL_WIDTH, MODEL_WIDTH), MODEL_WIDTH ** -0.5, 0.1875, ((1, 2),))
    w_value_proc = bell_draw(key_of[9], (MODEL_WIDTH, MODEL_WIDTH), MODEL_WIDTH ** -0.5, 0.1875, ((1, 2),))
    w_out_proc = bell_draw(key_of[10], (MODEL_WIDTH, MODEL_WIDTH), MODEL_WIDTH ** -0.5, 0.1875, ((0, 2),))
    send_rows = plant(jax.random.randint(key_of[11], (GROUPS, NEIGH, CAP), 0, GRID_REG), jax.random.fold_in(key_of[11], 1), 0, GRID_REG - 1).astype(jnp.int32)
    edge_senders = draw_edge_senders(jax.random.fold_in(key_of[14], 71), 0)
    edge_mask = draw_edge_mask(jax.random.fold_in(key_of[14], 71), 0)
    return {"grid_fields": grid_fields, "mesh_state": mesh_state, "w_embed": w_embed, "w_query_enc": w_query_enc, "w_key_enc": w_key_enc, "w_value_enc": w_value_enc, "w_out_enc": w_out_enc, "w_query_proc": w_query_proc, "w_key_proc": w_key_proc, "w_value_proc": w_value_proc, "w_out_proc": w_out_proc, "send_rows": send_rows, "edge_senders": edge_senders, "edge_mask": edge_mask}


def normalize(values):
    values = values.astype(jnp.float32)
    centred = values - lax.optimization_barrier(jnp.mean(values, axis=-1, keepdims=True))
    spread = lax.optimization_barrier(jnp.mean(centred * centred, axis=-1, keepdims=True))
    return centred * lax.rsqrt(spread + 1e-05)

def neighbour_offset(slot):
    return (slot // 2 + 1) * (1 if slot % 2 == 0 else -1)

def reference(grid_fields, mesh_state, w_embed, w_query_enc, w_key_enc, w_value_enc, w_out_enc, w_query_proc, w_key_proc, w_value_proc, w_out_proc, send_rows, edge_senders, edge_mask):
    logit_scale_factor = 1.0 / math.sqrt(HS)
    fields_regions = grid_fields.reshape(CH, GROUPS, GRID_REG).transpose(1, 0, 2)

    def embed_region(fields_block):
        projected = lax.dot_general(fields_block, w_embed, (((0,), (0,)), ((), ())), preferred_element_type=jnp.float32)
        embedded = normalize(projected).astype(jnp.bfloat16)
        keys_block = jnp.dot(embedded, w_key_enc, preferred_element_type=jnp.float32).astype(jnp.bfloat16)
        values_block = jnp.dot(embedded, w_value_enc, preferred_element_type=jnp.float32).astype(jnp.bfloat16)
        return (keys_block, values_block)
    grid_keys, grid_values = lax.map(embed_region, fields_regions)
    grid_keys = grid_keys.reshape(GRID_POINTS, MODEL_WIDTH)
    grid_values = grid_values.reshape(GRID_POINTS, MODEL_WIDTH)
    mesh_regions = mesh_state.reshape(GROUPS, REGION_MESH_NODES, MODEL_WIDTH)
    sender_regions = edge_senders.reshape(GROUPS, REGION_MESH_NODES, FAN)
    mask_regions = edge_mask.reshape(GROUPS, REGION_MESH_NODES, FAN)
    offsets = jnp.array([neighbour_offset(slot) for slot in range(NEIGH)], dtype=jnp.int32)

    def region_layer(inputs):
        region_index, mesh_rows, senders_block, mask_block = inputs
        local_ids = region_index * GRID_REG + jnp.arange(GRID_REG, dtype=jnp.int32)
        source_regions = jnp.mod(region_index - offsets, GROUPS).astype(jnp.int32)
        listed = send_rows[source_regions, jnp.arange(NEIGH, dtype=jnp.int32), :]
        remote_ids = (source_regions[:, None] * GRID_REG + listed).reshape(-1)
        table_ids = jnp.concatenate([local_ids, remote_ids.astype(jnp.int32)]).astype(jnp.int32)
        sender_ids = table_ids[senders_block]
        keys_edge = grid_keys[sender_ids].reshape(REGION_MESH_NODES, FAN, HEADS, HS).astype(jnp.float32)
        values_edge = grid_values[sender_ids].reshape(REGION_MESH_NODES, FAN, HEADS, HS).astype(jnp.float32)
        queries = jnp.dot(normalize(mesh_rows).astype(jnp.bfloat16), w_query_enc, preferred_element_type=jnp.float32).astype(jnp.bfloat16)
        queries = queries.reshape(REGION_MESH_NODES, HEADS, HS).astype(jnp.float32)
        scores = jnp.einsum('nhd,nfhd->nhf', queries, keys_edge) * logit_scale_factor
        weights = jnp.where(mask_block[:, None, :] > 0, jnp.exp(scores), jnp.float32(0.0))
        enc_probs = (weights / lax.optimization_barrier(jnp.sum(weights, axis=-1, keepdims=True))).astype(jnp.bfloat16)
        enc_context = jnp.einsum('nhf,nfhd->nhd', enc_probs.astype(jnp.float32), values_edge).astype(jnp.bfloat16).reshape(REGION_MESH_NODES, MODEL_WIDTH)
        hidden = mesh_rows.astype(jnp.float32) + jnp.dot(enc_context, w_out_enc, preferred_element_type=jnp.float32)
        normed = normalize(hidden).astype(jnp.bfloat16)
        processor_queries = jnp.dot(normed, w_query_proc, preferred_element_type=jnp.float32).astype(jnp.bfloat16).reshape(REGION_MESH_NODES, HEADS, HS)
        processor_keys = jnp.dot(normed, w_key_proc, preferred_element_type=jnp.float32).astype(jnp.bfloat16).reshape(REGION_MESH_NODES, HEADS, HS)
        processor_values = jnp.dot(normed, w_value_proc, preferred_element_type=jnp.float32).astype(jnp.bfloat16).reshape(REGION_MESH_NODES, HEADS, HS)
        processor_scores = jnp.einsum('pws,iws->wpi', processor_queries.astype(jnp.float32), processor_keys.astype(jnp.float32)) * logit_scale_factor
        layer_weights = jnp.exp(processor_scores)
        processor_probabilities = (layer_weights / lax.optimization_barrier(jnp.sum(layer_weights, axis=-1, keepdims=True))).astype(jnp.bfloat16)
        processor_context = jnp.einsum('beq,qbo->ebo', processor_probabilities.astype(jnp.float32), processor_values.astype(jnp.float32)).astype(jnp.bfloat16).reshape(REGION_MESH_NODES, MODEL_WIDTH)
        return (hidden + jnp.dot(processor_context, w_out_proc, preferred_element_type=jnp.float32)).astype(jnp.bfloat16)
    region_ids = jnp.arange(GROUPS, dtype=jnp.int32)
    layer_out = lax.map(region_layer, (region_ids, mesh_regions, sender_regions, mask_regions))
    return layer_out.reshape(MESH_NODES, MODEL_WIDTH)
```

```python
import functools
import math

import jax
import jax.numpy as jnp
from jax import lax
from jax.experimental import pallas as pl
from jax.experimental.pallas import tpu as pltpu
from jax.sharding import PartitionSpec as P

HEADS = 16
HS = 64
NEIGH = 4
F32 = jnp.float32
BF16 = jnp.bfloat16
MESH = pl.DeviceIdType.MESH
LANES = 128
LOG2E = math.log2(math.e)
NN = (((1,), (0,)), ((), ()))
NT = (((1,), (1,)), ((), ()))


def offset_of(slot):
    return (slot // 2 + 1) * (1 if slot % 2 == 0 else -1)


def dot(a, b, dims=NN):
    return lax.dot_general(a, b, dims, preferred_element_type=F32)


def split(x):
    high = x.astype(BF16)
    return high, (x - high.astype(F32)).astype(BF16)


def normalize(x):
    centred = x - jnp.mean(x, axis=-1, keepdims=True)
    spread = jnp.mean(centred * centred, axis=-1, keepdims=True)
    return centred * lax.rsqrt(spread + 1e-05)


def iota(shape, axis):
    return lax.broadcasted_iota(jnp.int32, shape, axis)


def kernel(
    fields, mesh_state, w_embed, w_q, w_k, w_v, w_o, p_q, p_k, p_v, p_o, send_rows, senders, mask,
    out,
    own_v, mesh_v, embed_v, wq_v, wk_v, wv_v, wo_v, pq_v, pk_v, pv_v, po_v, rows_v, send_v, mask_v,
    other_v, listed, received, table, bias, weights_k, weights_v, queries, hidden, sums_out, sums_in,
    context, last_out, last_in,
    load_sem, half_sem, list_send, list_recv, sum_send, sum_recv, last_sem,
):
    n = lax.axis_size("nodes")
    region, core = lax.axis_index("nodes"), lax.axis_index("heads")
    twin = {"nodes": region, "heads": 1 - core}
    ch, half = fields.shape
    nodes, width = mesh_state.shape
    fan = senders.shape[1]
    cols = w_q.shape[1]
    pairs = cols // LANES
    cap = send_rows.shape[2]
    points = 2 * half
    remote = NEIGH * cap
    own_rows = nodes // 2
    chunk = width // 4

    def neighbour(slot, other):
        place = lax.rem(region + (offset_of(slot) + n), n)
        return {"nodes": place, "heads": 1 - core if other else core}

    barrier = pltpu.get_barrier_semaphore()
    pl.semaphore_signal(barrier, inc=1, device_id=twin, device_id_type=MESH)
    for slot in range(NEIGH):
        for other in range(2):
            pl.semaphore_signal(
                barrier, inc=1, device_id=neighbour(slot, other), device_id_type=MESH
            )

    loads = {}
    pieces = [
        (fields, own_v), (send_rows, rows_v), (w_embed, embed_v), (w_k, wk_v), (w_v, wv_v),
        (senders, send_v), (mask, mask_v), (mesh_state, mesh_v), (w_q, wq_v), (w_o, wo_v),
        (p_q, pq_v), (p_k, pk_v), (p_v, pv_v), (p_o, po_v),
    ]
    for index, (source, target) in enumerate(pieces):
        loads[id(target)] = pltpu.make_async_copy(source, target, load_sem.at[index])
        loads[id(target)].start()

    def loaded(*targets):
        for target in targets:
            loads[id(target)].wait()

    loaded(own_v, rows_v)
    widen = (iota((LANES, ch), 0) == iota((LANES, ch), 1)).astype(BF16)
    own = dot(widen, own_v[...]).astype(BF16)
    table[0:LANES, 0:half] = own
    table[LANES : 2 * LANES, 0:half] = own
    rows = rows_v[0]
    wanted = jnp.concatenate([rows[j : j + 1, :] for j in range(NEIGH)], axis=1) - core * half
    pick = (iota((half, remote), 0) == wanted).astype(BF16)
    listed[...] = dot(own, pick).T.astype(BF16)
    pl.semaphore_wait(barrier, 1 + 2 * NEIGH)
    half_copy = pltpu.make_async_remote_copy(
        src_ref=fields, dst_ref=other_v, send_sem=half_sem.at[0], recv_sem=half_sem.at[1],
        device_id=twin, device_id_type=MESH,
    )
    half_copy.start()
    list_copies = []
    for slot in range(NEIGH):
        for other in range(2):
            part = pl.ds(slot * cap, cap)
            list_copies.append(
                pltpu.make_async_remote_copy(
                    src_ref=listed.at[part], dst_ref=received.at[other, part],
                    send_sem=list_send.at[2 * slot + other],
                    recv_sem=list_recv.at[2 * slot + other],
                    device_id=neighbour(slot, other), device_id_type=MESH,
                )
            )
            list_copies[-1].start()

    loaded(embed_v)
    embed = dot(widen, embed_v[...])
    embed = embed - jnp.mean(embed, axis=-1, keepdims=True)
    embed = jnp.concatenate(split(embed), axis=0)
    gram = dot(embed, embed, NT) * (1.0 / width)
    gram = gram[:LANES] + gram[LANES:]
    gram = jnp.concatenate(split(gram[:, :LANES] + gram[:, LANES:]), axis=1)
    loaded(wk_v, wv_v)
    for weight, target in ((wk_v, weights_k), (wv_v, weights_v)):
        both = dot(embed, weight[...])
        high, low = split(both[:LANES] + both[LANES:])
        target[0] = high
        target[1] = low

    loaded(send_v, mask_v)
    block = 32
    place = iota((1, points), 1)
    place = jnp.where(place < half, place + core * half, place - core * half)
    place = jnp.concatenate([place, iota((1, remote), 1) + points], axis=1)

    def count(step, carry):
        part = pl.ds(pl.multiple_of(step * block, block), block)
        live = jnp.where(mask_v[part, :] > 0, send_v[part, :], -1)
        total = jnp.zeros((block, points + remote), F32)
        for slot in range(fan):
            total += (live[:, slot : slot + 1] == place).astype(F32)
        bias[part, :] = jnp.where(total > 0, jnp.log2(jnp.maximum(total, 1.0)), -1e30)
        return carry

    lax.fori_loop(0, nodes // block, count, 0)

    loaded(mesh_v, wq_v)
    normed = normalize(mesh_v[...].astype(F32)).astype(BF16)
    enc_queries = dot(normed, wq_v[...]).astype(BF16)
    low_lanes = iota((nodes, LANES), 1) < HS
    for pair in range(pairs):
        lanes = slice(pair * LANES, (pair + 1) * LANES)
        two = enc_queries[:, lanes]
        even = jnp.where(low_lanes, two, jnp.zeros_like(two))
        odd = jnp.where(low_lanes, jnp.zeros_like(two), two)
        two = jnp.concatenate([even, odd], axis=0)
        spread = dot(two, weights_k[0, :, lanes], NT) + dot(two, weights_k[1, :, lanes], NT)
        high, low = split(spread)
        queries[pair, :, 0:LANES] = high
        queries[pair, :, LANES : 2 * LANES] = low

    half_copy.wait()
    other = dot(widen, other_v[...]).astype(BF16)
    table[0:LANES, half:points] = other
    table[LANES : 2 * LANES, half:points] = other
    for copy in list_copies:
        copy.wait()
    far = (received[0].astype(F32) + received[1].astype(F32)).T.astype(BF16)
    table[0:LANES, points : points + remote] = far
    table[LANES : 2 * LANES, points : points + remote] = far
    squares = dot(gram, table[...]) * table[0:LANES, :].astype(F32)
    squares = jnp.maximum(jnp.sum(squares, axis=0, keepdims=True), 0.0)
    inverse = lax.rsqrt(squares + 1e-05)
    logit_scale = inverse * (LOG2E / math.sqrt(HS))

    loaded(wo_v)
    points_last = table[0:LANES, :]
    edges = bias[...]
    edges = jnp.concatenate([edges, edges], axis=0)
    for pair in range(pairs):
        lanes = slice(pair * LANES, (pair + 1) * LANES)
        logits = dot(queries[pair], table[...]) * logit_scale + edges
        logits = jnp.exp2(logits - jnp.max(logits, axis=-1, keepdims=True))
        total = jnp.sum(logits, axis=-1, keepdims=True)
        mixed = dot((logits * inverse).astype(BF16), points_last, NT) / total
        high, low = split(mixed)
        both = (
            dot(high, weights_v[0, :, lanes])
            + dot(high, weights_v[1, :, lanes])
            + dot(low, weights_v[0, :, lanes])
        )
        context[:, lanes] = jnp.where(low_lanes, both[:nodes], both[nodes:]).astype(BF16)

    sum_copies = []
    for step in range(4):
        lanes = slice(step * chunk, (step + 1) * chunk)
        part = dot(context[...], wo_v[:, lanes])
        sums_out[step] = part.astype(BF16)
        sum_copies.append(
            pltpu.make_async_remote_copy(
                src_ref=sums_out.at[step], dst_ref=sums_in.at[step],
                send_sem=sum_send.at[step], recv_sem=sum_recv.at[step],
                device_id=twin, device_id_type=MESH,
            )
        )
        sum_copies[-1].start()
        hidden[:, lanes] = mesh_v[:, lanes].astype(F32) + part
    for step in range(4):
        lanes = slice(step * chunk, (step + 1) * chunk)
        sum_copies[step].wait()
        hidden[:, lanes] += sums_in[step].astype(F32)

    normed = normalize(hidden[...]).astype(BF16)
    loaded(pq_v, pk_v, pv_v)
    proc_q = dot(normed, pq_v[...]).astype(BF16)
    proc_k = dot(normed, pk_v[...]).astype(BF16)
    proc_v = dot(normed, pv_v[...]).astype(BF16)
    for pair in range(pairs):
        lanes = slice(pair * LANES, (pair + 1) * LANES)
        two = proc_q[:, lanes]
        even = jnp.where(low_lanes, two, jnp.zeros_like(two))
        odd = jnp.where(low_lanes, jnp.zeros_like(two), two)
        two = jnp.concatenate([even, odd], axis=0)
        logits = dot(two, proc_k[:, lanes], NT) * (LOG2E / math.sqrt(HS))
        logits = jnp.exp2(logits - jnp.max(logits, axis=-1, keepdims=True))
        probs = (logits / jnp.sum(logits, axis=-1, keepdims=True)).astype(BF16)
        both = dot(probs, proc_v[:, lanes])
        context[:, lanes] = jnp.where(low_lanes, both[:nodes], both[nodes:]).astype(BF16)

    loaded(po_v)
    theirs = pl.ds(pl.multiple_of((1 - core) * own_rows, own_rows), own_rows)
    mine = pl.ds(pl.multiple_of(core * own_rows, own_rows), own_rows)
    last_out[...] = dot(context[theirs, :], po_v[...]).astype(BF16)
    last = pltpu.make_async_remote_copy(
        src_ref=last_out, dst_ref=last_in, send_sem=last_sem.at[0], recv_sem=last_sem.at[1],
        device_id=twin, device_id_type=MESH,
    )
    last.start()
    part = hidden[mine, :] + dot(context[mine, :], po_v[...])
    last.wait()
    out[...] = (part + last_in[...].astype(F32)).astype(BF16)


def local(*args):
    fields, mesh_state = args[0], args[1]
    send_rows, senders = args[11], args[12]
    ch, half = fields.shape
    nodes, width = mesh_state.shape
    cols = args[3].shape[1]
    pairs = cols // LANES
    remote = send_rows.shape[1] * send_rows.shape[2]
    columns = 2 * half + remote
    copies = [pltpu.VMEM(x.shape, x.dtype) for x in args]
    buffers = [
        pltpu.VMEM((ch, half), BF16),
        pltpu.VMEM((remote, LANES), BF16),
        pltpu.VMEM((2, remote, LANES), BF16),
        pltpu.VMEM((2 * LANES, columns), BF16),
        pltpu.VMEM((nodes, columns), F32),
        pltpu.VMEM((2, LANES, cols), BF16),
        pltpu.VMEM((2, LANES, cols), BF16),
        pltpu.VMEM((pairs, 2 * nodes, 2 * LANES), BF16),
        pltpu.VMEM((nodes, width), F32),
        pltpu.VMEM((4, nodes, width // 4), BF16),
        pltpu.VMEM((4, nodes, width // 4), BF16),
        pltpu.VMEM((nodes, cols), BF16),
        pltpu.VMEM((nodes // 2, width), BF16),
        pltpu.VMEM((nodes // 2, width), BF16),
    ]
    semaphores = [
        pltpu.SemaphoreType.DMA((len(args),)),
        pltpu.SemaphoreType.DMA((2,)),
        pltpu.SemaphoreType.DMA((2 * NEIGH,)),
        pltpu.SemaphoreType.DMA((2 * NEIGH,)),
        pltpu.SemaphoreType.DMA((4,)),
        pltpu.SemaphoreType.DMA((4,)),
        pltpu.SemaphoreType.DMA((2,)),
    ]
    return pl.pallas_call(
        kernel,
        out_shape=jax.ShapeDtypeStruct((nodes // 2, width), BF16),
        in_specs=[pl.BlockSpec(memory_space=pl.ANY)] * len(args),
        out_specs=pl.BlockSpec(memory_space=pltpu.VMEM),
        scratch_shapes=copies + buffers + semaphores,
        compiler_params=pltpu.CompilerParams(
            collective_id=0, has_side_effects=True, vmem_limit_bytes=48 * 1024 * 1024
        ),
        cost_estimate=pl.CostEstimate(
            flops=3_000_000_000, bytes_accessed=9_500_000, transcendentals=800_000
        ),
        name="encode_and_process",
    )(*args)


def solution(mesh):
    return jax.shard_map(
        local,
        mesh=mesh,
        in_specs=(
            P(None, ("nodes", "heads")),
            P("nodes", None),
            P(),
            P(None, "heads"),
            P(None, "heads"),
            P(None, "heads"),
            P("heads", None),
            P(None, "heads"),
            P(None, "heads"),
            P(None, "heads"),
            P("heads", None),
            P("nodes", None, None),
            P("nodes", None),
            P("nodes", None),
        ),
        out_specs=P(("nodes", "heads"), None),
        check_vma=False,
    )
```

```python
import math

import jax
import jax.numpy as jnp
from jax import lax
from jax.experimental import pallas as pl
from jax.experimental.pallas import tpu as pltpu
from jax.sharding import PartitionSpec as P

HEADS = 16
HS = 64
NEIGH = 4
F32 = jnp.float32
BF16 = jnp.bfloat16
MESH = pl.DeviceIdType.MESH
LANES = 128
LOG2E = math.log2(math.e)
NN = (((1,), (0,)), ((), ()))
NT = (((1,), (1,)), ((), ()))


def offset_of(slot):
    return (slot // 2 + 1) * (1 if slot % 2 == 0 else -1)


def dot(a, b, dims=NN):
    return lax.dot_general(a, b, dims, preferred_element_type=F32)


def split(x):
    high = x.astype(BF16)
    return high, (x - high.astype(F32)).astype(BF16)


def normalize(x):
    centred = x - jnp.mean(x, axis=-1, keepdims=True)
    spread = jnp.mean(centred * centred, axis=-1, keepdims=True)
    return centred * lax.rsqrt(spread + 1e-05)


def iota(shape, axis):
    return lax.broadcasted_iota(jnp.int32, shape, axis)


def kernel(
    fields, mesh_state, w_embed, w_q, w_k, w_v, w_o, p_q, p_k, p_v, p_o, send_rows, senders, mask,
    out,
    own_v, mesh_v, embed_v, wq_v, wk_v, wv_v, wo_v, pq_v, pk_v, pv_v, po_v, rows_v, send_v, mask_v,
    other_v, listed, received, table, bias, weights_k, weights_v, queries, hidden, sums_out, sums_in,
    context, last_out, last_in,
    load_sem, half_sem, list_send, list_recv, sum_send, sum_recv, last_sem,
):
    n = lax.axis_size("nodes")
    region, core = lax.axis_index("nodes"), lax.axis_index("heads")
    twin = {"nodes": region, "heads": 1 - core}
    ch, half = fields.shape
    nodes, width = mesh_state.shape
    fan = senders.shape[0]
    cols = w_q.shape[1]
    pairs = cols // LANES
    cap = send_rows.shape[2]
    points = 2 * half
    remote = NEIGH * cap
    own_rows = nodes // 2
    chunk = width // 4

    def neighbour(slot, other):
        place = lax.rem(region + (offset_of(slot) + n), n)
        return {"nodes": place, "heads": 1 - core if other else core}

    barrier = pltpu.get_barrier_semaphore()
    pl.semaphore_signal(barrier, inc=1, device_id=twin, device_id_type=MESH)
    for slot in range(NEIGH):
        for other in range(2):
            pl.semaphore_signal(
                barrier, inc=1, device_id=neighbour(slot, other), device_id_type=MESH
            )

    loads = {}
    pieces = [
        (fields, own_v), (send_rows, rows_v), (w_embed, embed_v), (w_k, wk_v), (w_v, wv_v),
        (senders, send_v), (mask, mask_v), (mesh_state, mesh_v), (w_q, wq_v), (w_o, wo_v),
        (p_q, pq_v), (p_k, pk_v), (p_v, pv_v), (p_o, po_v),
    ]
    for index, (source, target) in enumerate(pieces):
        loads[id(target)] = pltpu.make_async_copy(source, target, load_sem.at[index])
        loads[id(target)].start()

    def loaded(*targets):
        for target in targets:
            loads.pop(id(target)).wait()

    loaded(own_v, rows_v)
    widen = (iota((LANES, ch), 0) == iota((LANES, ch), 1)).astype(BF16)
    own = dot(widen, own_v[...]).astype(BF16)
    table[0:LANES, 0:half] = own
    table[LANES : 2 * LANES, 0:half] = own
    rows = rows_v[0]
    wanted = jnp.concatenate([rows[j : j + 1, :] for j in range(NEIGH)], axis=1) - core * half
    pick = (iota((half, remote), 0) == wanted).astype(BF16)
    listed[...] = dot(own, pick).T.astype(BF16)
    pl.semaphore_wait(barrier, 1 + 2 * NEIGH)
    half_copy = pltpu.make_async_remote_copy(
        src_ref=fields, dst_ref=other_v, send_sem=half_sem.at[0], recv_sem=half_sem.at[1],
        device_id=twin, device_id_type=MESH,
    )
    half_copy.start()
    list_copies = []
    for slot in range(NEIGH):
        for other in range(2):
            part = pl.ds(slot * cap, cap)
            list_copies.append(
                pltpu.make_async_remote_copy(
                    src_ref=listed.at[part], dst_ref=received.at[other, part],
                    send_sem=list_send.at[2 * slot + other],
                    recv_sem=list_recv.at[2 * slot + other],
                    device_id=neighbour(slot, other), device_id_type=MESH,
                )
            )
            list_copies[-1].start()

    loaded(embed_v)
    embed = dot(widen, embed_v[...])
    embed = embed - jnp.mean(embed, axis=-1, keepdims=True)
    embed = jnp.concatenate(split(embed), axis=0)
    gram = dot(embed, embed, NT) * (1.0 / width)
    gram = gram[:LANES] + gram[LANES:]
    gram = jnp.concatenate(split(gram[:, :LANES] + gram[:, LANES:]), axis=1)
    loaded(wk_v, wv_v)
    for weight, target in ((wk_v, weights_k), (wv_v, weights_v)):
        both = dot(embed, weight[...])
        high, low = split(both[:LANES] + both[LANES:])
        target[0] = high
        target[1] = low

    loaded(send_v, mask_v)
    live = jnp.where(mask_v[...] > 0, send_v[...], -1)
    for step in range((points + remote) // LANES):
        start = step * LANES
        if start < points:
            start = lax.rem(start + core * half, points)
        total = jnp.zeros((LANES, nodes), F32)
        for slot in range(fan):
            total += (live[slot : slot + 1, :] - start == iota((LANES, nodes), 0)).astype(F32)
        total = jnp.where(total > 0, jnp.log2(jnp.maximum(total, 1.0)), -1e30)
        bias[:, step * LANES : (step + 1) * LANES] = total.T

    loaded(mesh_v, wq_v)
    normed = normalize(mesh_v[...].astype(F32)).astype(BF16)
    enc_queries = dot(normed, wq_v[...]).astype(BF16)
    low_lanes = iota((nodes, LANES), 1) < HS
    for pair in range(pairs):
        lanes = slice(pair * LANES, (pair + 1) * LANES)
        two = enc_queries[:, lanes]
        even = jnp.where(low_lanes, two, jnp.zeros_like(two))
        odd = jnp.where(low_lanes, jnp.zeros_like(two), two)
        two = jnp.concatenate([even, odd], axis=0)
        spread = dot(two, weights_k[0, :, lanes], NT) + dot(two, weights_k[1, :, lanes], NT)
        high, low = split(spread)
        queries[pair, :, 0:LANES] = high
        queries[pair, :, LANES : 2 * LANES] = low

    half_copy.wait()
    other = dot(widen, other_v[...]).astype(BF16)
    table[0:LANES, half:points] = other
    table[LANES : 2 * LANES, half:points] = other
    for copy in list_copies:
        copy.wait()
    far = (received[0].astype(F32) + received[1].astype(F32)).T.astype(BF16)
    table[0:LANES, points : points + remote] = far
    table[LANES : 2 * LANES, points : points + remote] = far
    squares = dot(gram, table[...]) * table[0:LANES, :].astype(F32)
    squares = jnp.maximum(jnp.sum(squares, axis=0, keepdims=True), 0.0)
    inverse = lax.rsqrt(squares + 1e-05)
    logit_scale = inverse * (LOG2E / math.sqrt(HS))

    loaded(wo_v)
    points_last = table[0:LANES, :]
    edges = bias[...]
    edges = jnp.concatenate([edges, edges], axis=0)
    for pair in range(pairs):
        lanes = slice(pair * LANES, (pair + 1) * LANES)
        logits = dot(queries[pair], table[...]) * logit_scale + edges
        logits = jnp.exp2(logits - jnp.max(logits, axis=-1, keepdims=True))
        total = jnp.sum(logits, axis=-1, keepdims=True)
        mixed = dot((logits * inverse).astype(BF16), points_last, NT) / total
        high, low = split(mixed)
        both = (
            dot(high, weights_v[0, :, lanes])
            + dot(high, weights_v[1, :, lanes])
            + dot(low, weights_v[0, :, lanes])
        )
        context[:, lanes] = jnp.where(low_lanes, both[:nodes], both[nodes:]).astype(BF16)

    sum_copies = []
    for step in range(4):
        lanes = slice(step * chunk, (step + 1) * chunk)
        part = dot(context[...], wo_v[:, lanes])
        sums_out[step] = part.astype(BF16)
        sum_copies.append(
            pltpu.make_async_remote_copy(
                src_ref=sums_out.at[step], dst_ref=sums_in.at[step],
                send_sem=sum_send.at[step], recv_sem=sum_recv.at[step],
                device_id=twin, device_id_type=MESH,
            )
        )
        sum_copies[-1].start()
        hidden[:, lanes] = mesh_v[:, lanes].astype(F32) + part
    for step in range(4):
        lanes = slice(step * chunk, (step + 1) * chunk)
        sum_copies[step].wait()
        hidden[:, lanes] += sums_in[step].astype(F32)

    normed = normalize(hidden[...]).astype(BF16)
    loaded(pq_v, pk_v, pv_v)
    proc_q = dot(normed, pq_v[...]).astype(BF16)
    proc_k = dot(normed, pk_v[...]).astype(BF16)
    proc_v = dot(normed, pv_v[...]).astype(BF16)
    for pair in range(pairs):
        lanes = slice(pair * LANES, (pair + 1) * LANES)
        two = proc_q[:, lanes]
        even = jnp.where(low_lanes, two, jnp.zeros_like(two))
        odd = jnp.where(low_lanes, jnp.zeros_like(two), two)
        two = jnp.concatenate([even, odd], axis=0)
        logits = dot(two, proc_k[:, lanes], NT) * (LOG2E / math.sqrt(HS))
        logits = jnp.exp2(logits - jnp.max(logits, axis=-1, keepdims=True))
        probs = (logits / jnp.sum(logits, axis=-1, keepdims=True)).astype(BF16)
        both = dot(probs, proc_v[:, lanes])
        context[:, lanes] = jnp.where(low_lanes, both[:nodes], both[nodes:]).astype(BF16)

    loaded(po_v)
    theirs = pl.ds(pl.multiple_of((1 - core) * own_rows, own_rows), own_rows)
    mine = pl.ds(pl.multiple_of(core * own_rows, own_rows), own_rows)
    last_out[...] = dot(context[theirs, :], po_v[...]).astype(BF16)
    last = pltpu.make_async_remote_copy(
        src_ref=last_out, dst_ref=last_in, send_sem=last_sem.at[0], recv_sem=last_sem.at[1],
        device_id=twin, device_id_type=MESH,
    )
    last.start()
    part = hidden[mine, :] + dot(context[mine, :], po_v[...])
    last.wait()
    out[...] = (part + last_in[...].astype(F32)).astype(BF16)


def local(*args):
    args = args[:12] + (args[12].T, args[13].T)
    fields, mesh_state = args[0], args[1]
    send_rows = args[11]
    ch, half = fields.shape
    nodes, width = mesh_state.shape
    cols = args[3].shape[1]
    pairs = cols // LANES
    remote = send_rows.shape[1] * send_rows.shape[2]
    columns = 2 * half + remote
    copies = [pltpu.VMEM(x.shape, x.dtype) for x in args]
    buffers = [
        pltpu.VMEM((ch, half), BF16),
        pltpu.VMEM((remote, LANES), BF16),
        pltpu.VMEM((2, remote, LANES), BF16),
        pltpu.VMEM((2 * LANES, columns), BF16),
        pltpu.VMEM((nodes, columns), F32),
        pltpu.VMEM((2, LANES, cols), BF16),
        pltpu.VMEM((2, LANES, cols), BF16),
        pltpu.VMEM((pairs, 2 * nodes, 2 * LANES), BF16),
        pltpu.VMEM((nodes, width), F32),
        pltpu.VMEM((4, nodes, width // 4), BF16),
        pltpu.VMEM((4, nodes, width // 4), BF16),
        pltpu.VMEM((nodes, cols), BF16),
        pltpu.VMEM((nodes // 2, width), BF16),
        pltpu.VMEM((nodes // 2, width), BF16),
    ]
    semaphores = [
        pltpu.SemaphoreType.DMA((len(args),)),
        pltpu.SemaphoreType.DMA((2,)),
        pltpu.SemaphoreType.DMA((2 * NEIGH,)),
        pltpu.SemaphoreType.DMA((2 * NEIGH,)),
        pltpu.SemaphoreType.DMA((4,)),
        pltpu.SemaphoreType.DMA((4,)),
        pltpu.SemaphoreType.DMA((2,)),
    ]
    return pl.pallas_call(
        kernel,
        out_shape=jax.ShapeDtypeStruct((nodes // 2, width), BF16),
        in_specs=[pl.BlockSpec(memory_space=pltpu.HBM)] * len(args),
        out_specs=pl.BlockSpec(memory_space=pltpu.VMEM),
        scratch_shapes=copies + buffers + semaphores,
        compiler_params=pltpu.CompilerParams(
            collective_id=0, has_side_effects=True, vmem_limit_bytes=56 * 1024 * 1024
        ),
        cost_estimate=pl.CostEstimate(
            flops=3_000_000_000, bytes_accessed=9_500_000, transcendentals=800_000
        ),
        name="encode_and_process",
    )(*args)


def solution(mesh):
    return jax.shard_map(
        local,
        mesh=mesh,
        in_specs=(
            P(None, ("nodes", "heads")),
            P("nodes", None),
            P(),
            P(None, "heads"),
            P(None, "heads"),
            P(None, "heads"),
            P("heads", None),
            P(None, "heads"),
            P(None, "heads"),
            P(None, "heads"),
            P("heads", None),
            P("nodes", None, None),
            P("nodes", None),
            P("nodes", None),
        ),
        out_specs=P(("nodes", "heads"), None),
        check_vma=False,
    )
```

```python
import functools
import math

import jax
import jax.numpy as jnp
from jax import lax
from jax.experimental import pallas as pl
from jax.experimental.pallas import tpu as pltpu
from jax.sharding import PartitionSpec as P

HEADS = 16
HS = 64
NEIGH = 4
STEPS = 4
F32 = jnp.float32
BF16 = jnp.bfloat16
MESH = pl.DeviceIdType.MESH
LANES = 128
LOG2E = math.log2(math.e)
NN = (((1,), (0,)), ((), ()))
NT = (((1,), (1,)), ((), ()))


def offset_of(slot):
    return (slot // 2 + 1) * (1 if slot % 2 == 0 else -1)


def dot(a, b, dims=NN):
    return lax.dot_general(a, b, dims, preferred_element_type=F32)


def split(x):
    high = x.astype(BF16)
    return high, (x - high.astype(F32)).astype(BF16)


def normalize(x):
    centred = x - jnp.mean(x, axis=-1, keepdims=True)
    spread = jnp.mean(centred * centred, axis=-1, keepdims=True)
    return centred * lax.rsqrt(spread + 1e-05)


def iota(shape, axis):
    return lax.broadcasted_iota(jnp.int32, shape, axis)


def kernel(
    fields, mesh_state, w_embed, w_q, w_k, w_v, w_o, p_q, p_k, p_v, p_o, send_rows, senders, mask,
    out,
    own_v, mesh_v, embed_v, wq_v, wk_v, wv_v, wo_v, pq_v, pk_v, pv_v, po_v, rows_v, send_v, mask_v,
    other_v, listed, received, table, last, values, bias, queries, hidden, sums_out, sums_in,
    context, tail, last_out, last_in,
    load_sem, half_sem, list_send, list_recv, sum_send, sum_recv, last_send, last_recv,
    wrap_sem,
):
    n = lax.axis_size("nodes")
    region, core = lax.axis_index("nodes"), lax.axis_index("heads")
    twin = {"nodes": region, "heads": 1 - core}
    ch, half = fields.shape
    nodes, width = mesh_state.shape
    fan = senders.shape[0]
    cols = w_q.shape[1]
    pairs = cols // LANES
    cap = send_rows.shape[2]
    points = 2 * half
    remote = NEIGH * cap
    own_rows = nodes // 2
    steps = sums_out.shape[0]
    chunk = width // steps
    exponent = LOG2E / math.sqrt(HS)

    def neighbour(slot, other):
        place = lax.rem(region + (offset_of(slot) + n), n)
        return {"nodes": place, "heads": 1 - core if other else core}

    loads = {}
    pieces = [
        (fields, own_v), (send_rows, rows_v), (w_embed, embed_v), (senders, send_v), (mask, mask_v),
        (mesh_state, mesh_v), (w_q, wq_v), (w_k, wk_v), (w_v, wv_v), (w_o, wo_v),
        (p_q, pq_v), (p_k, pk_v), (p_v, pv_v), (p_o, po_v),
    ]
    for index, (source, target) in enumerate(pieces):
        loads[id(target)] = pltpu.make_async_copy(source, target, load_sem.at[index])

    def loaded(*targets):
        for target in targets:
            loads.pop(id(target)).wait()

    for _, target in pieces[:3]:
        loads[id(target)].start()
    barrier = pltpu.get_barrier_semaphore()

    def greet(slot, semaphore):
        for other in range(2):
            pl.semaphore_signal(
                semaphore, inc=1, device_id=neighbour(slot, other), device_id_type=MESH
            )

    pl.semaphore_signal(barrier, inc=1, device_id=twin, device_id_type=MESH)
    for slot in range(NEIGH):
        if offset_of(slot) < 0:
            greet(slot, barrier)
        else:
            pl.when(region + offset_of(slot) < n)(functools.partial(greet, slot, barrier))
    late = sum((region + offset_of(slot) < 0).astype(jnp.int32) for slot in range(NEIGH))
    for _, target in pieces[3:]:
        loads[id(target)].start()

    loaded(own_v, rows_v)
    widen = (iota((LANES, ch), 0) == iota((LANES, ch), 1)).astype(BF16)
    own = dot(widen, own_v[...]).astype(BF16)
    rows = rows_v[0]
    wanted = jnp.concatenate([rows[j : j + 1, :] for j in range(NEIGH)], axis=1) - core * half
    pick = (iota((half, remote), 0) == wanted).astype(BF16)
    listed[...] = dot(own, pick).T.astype(BF16)

    pl.semaphore_wait(barrier, 1 + 2 * NEIGH - 2 * late)
    def list_copies(slot):
        part = pl.ds(slot * cap, cap)
        return [
            pltpu.make_async_remote_copy(
                src_ref=listed.at[part], dst_ref=received.at[other, part],
                send_sem=list_send.at[2 * slot + other], recv_sem=list_recv.at[2 * slot + other],
                device_id=neighbour(slot, other), device_id_type=MESH,
            )
            for other in range(2)
        ]

    def send_list(slot):
        for copy in list_copies(slot):
            copy.start()

    ahead = [slot for slot in range(NEIGH) if offset_of(slot) > 0]
    behind = [slot for slot in range(NEIGH) if offset_of(slot) < 0]
    for slot in ahead:
        send_list(slot)
    for slot in ahead:
        pl.when(region + offset_of(slot) >= n)(functools.partial(greet, slot, wrap_sem))
    for slot in behind:
        pl.when(region + offset_of(slot) >= 0)(functools.partial(send_list, slot))
    half_copy = pltpu.make_async_remote_copy(
        src_ref=fields, dst_ref=other_v, send_sem=half_sem.at[0], recv_sem=half_sem.at[1],
        device_id=twin, device_id_type=MESH,
    )
    half_copy.start()

    loaded(embed_v)
    embed = dot(widen, embed_v[...])
    embed = jnp.where(iota((LANES, 1), 0) == ch, 1.0, embed).astype(BF16)
    gram = dot(embed, embed, NT) * (1.0 / width)
    mean = gram[:, ch : ch + 1]
    gram = jnp.concatenate(split(gram - mean * gram[ch : ch + 1, :]), axis=1)

    def through(weight):
        both = dot(embed, weight[...])
        return split(both - mean * both[ch : ch + 1, :])

    def inverse_of(squares, axis):
        squares = jnp.maximum(jnp.sum(squares, axis=axis, keepdims=True), 0.0)
        return lax.rsqrt(squares + 1e-05)

    def place_half(block, first):
        twice = jnp.concatenate([block, block], axis=0)
        table[:, first : first + half] = twice
        block = block.astype(F32)
        squares = dot(gram, twice) * block
        last[first : first + half, :] = block.T.astype(BF16)
        return inverse_of(squares, 0), inverse_of(squares.T, 1)

    inverse, scale = place_half(own, 0)

    loaded(send_v, mask_v)
    spot = send_v[...]
    tiles = (points + remote) // LANES
    word = jnp.zeros_like(spot)
    for tile in range(tiles):
        word = jnp.where(spot >= tile * LANES, 1 << (6 * tile), word)
    word = jnp.where(mask_v[...] > 0, word, 0)
    spot = spot & (LANES - 1)
    down = iota((LANES, nodes), 0)
    counts = jnp.zeros((LANES, nodes), jnp.int32)
    for slot in range(fan):
        counts += jnp.where(spot[slot : slot + 1, :] == down, word[slot : slot + 1, :], 0)
    counts = counts.T
    for tile in range(tiles):
        total = ((counts >> (6 * tile)) & 63).astype(F32)
        total = jnp.where(total > 0, jnp.log2(jnp.maximum(total, 1.0)), -1e30)
        first = tile * LANES
        if first < points:
            first = lax.rem(first + core * half, points)
        bias[:, pl.ds(pl.multiple_of(first, LANES), LANES)] = total

    loaded(mesh_v, wq_v)
    normed = normalize(mesh_v[...].astype(F32)).astype(BF16)
    enc_queries = dot(normed, wq_v[...]).astype(BF16)

    loaded(wk_v)
    k_high, k_low = through(wk_v)
    low_lanes = iota((nodes, LANES), 1) < HS

    def lanes_of(pair):
        return slice(pair * LANES, (pair + 1) * LANES)

    def two_heads(rows):
        zeros = jnp.zeros_like(rows)
        even, odd = jnp.where(low_lanes, rows, zeros), jnp.where(low_lanes, zeros, rows)
        return jnp.concatenate([even, odd], axis=0)

    for pair in range(pairs):
        lanes = lanes_of(pair)
        two = two_heads(enc_queries[:, lanes])
        keys = jnp.concatenate([k_high[:, lanes], k_low[:, lanes]], axis=1)
        high, low = split(dot(jnp.concatenate([two, two], axis=1), keys, NT))
        queries[pair, :, 0:LANES] = high
        queries[pair, :, LANES : 2 * LANES] = low

    loaded(wv_v)
    v_both = jnp.concatenate(through(wv_v), axis=0)

    def values_of(rows, scale):
        return (dot(jnp.concatenate([rows, rows], axis=1), v_both) * scale).astype(BF16)

    def weigh(logits, edges, inverse):
        logits = logits * (inverse * exponent) + jnp.concatenate([edges, edges], axis=0)
        top = jnp.max(logits, axis=-1, keepdims=True)
        return top, jnp.exp2(logits - top).astype(BF16)

    def join_heads(rows):
        return jnp.where(low_lanes, rows[:nodes], rows[nodes:])

    def mix(probs, values):
        mixed = dot(probs, jnp.concatenate([values, jnp.ones_like(values)], axis=1))
        return join_heads(mixed[:, :LANES]), join_heads(mixed[:, LANES:])

    half_copy.wait()
    other_inverse, other_scale = place_half(dot(widen, other_v[...]).astype(BF16), half)
    inverse = jnp.concatenate([inverse, other_inverse], axis=1)
    values[0:half, :] = values_of(last[0:half, :], scale)
    values[half:points, :] = values_of(last[half:points, :], other_scale)
    near = []
    for pair in range(pairs):
        logits = dot(queries[pair], table[...])
        top, probs = weigh(logits, bias[:, 0:points], inverse)
        near.append((top, *mix(probs, values[:, lanes_of(pair)])))

    loaded(wo_v)
    pl.when(late > 0)(lambda: pl.semaphore_wait(wrap_sem, 2 * late))
    for slot in behind:
        pl.when(region + offset_of(slot) < 0)(functools.partial(send_list, slot))
    for slot in range(NEIGH):
        for copy in list_copies(slot):
            copy.wait()
    far = received[0] + received[1]
    far_twice = jnp.concatenate([far, far], axis=1)
    squares = dot(far_twice, gram, NT) * far.astype(F32)
    inverse = inverse_of(squares.T, 0)
    far_values = values_of(far, inverse_of(squares, 1))
    for pair in range(pairs):
        lanes = lanes_of(pair)
        logits = dot(queries[pair], far_twice, NT)
        top, probs = weigh(logits, bias[:, points : points + remote], inverse)
        mixed, total = mix(probs, far_values[:, lanes])
        near_top, near_mixed, near_total = near[pair]
        best = jnp.maximum(top, near_top)
        gain = join_heads(jnp.exp2(top - best))
        near_gain = join_heads(jnp.exp2(near_top - best))
        both = gain * mixed + near_gain * near_mixed
        context[:, lanes] = (both / (gain * total + near_gain * near_total)).astype(BF16)

    sum_copies = []
    for step in range(steps):
        lanes = slice(step * chunk, (step + 1) * chunk)
        part = dot(context[...], wo_v[:, lanes])
        sums_out[step] = part.astype(BF16)
        sum_copies.append(
            pltpu.make_async_remote_copy(
                src_ref=sums_out.at[step], dst_ref=sums_in.at[step],
                send_sem=sum_send.at[step], recv_sem=sum_recv.at[step],
                device_id=twin, device_id_type=MESH,
            )
        )
        sum_copies[-1].start()
        hidden[:, lanes] = mesh_v[:, lanes].astype(F32) + part
    loaded(pq_v, pk_v, pv_v, po_v)
    for step in range(steps):
        lanes = slice(step * chunk, (step + 1) * chunk)
        sum_copies[step].wait()
        hidden[:, lanes] += sums_in[step].astype(F32)

    normed = normalize(hidden[...]).astype(BF16)
    proc_q = dot(normed, pq_v[...]).astype(BF16)
    proc_k = dot(normed, pk_v[...]).astype(BF16)
    proc_v = dot(normed, pv_v[...]).astype(BF16)
    for pair in range(pairs):
        lanes = lanes_of(pair)
        logits = dot(two_heads(proc_q[:, lanes]), proc_k[:, lanes], NT) * exponent
        probs = jnp.exp2(logits - jnp.max(logits, axis=-1, keepdims=True)).astype(BF16)
        mixed, total = mix(probs, proc_v[:, lanes])
        context[:, lanes] = (mixed / total).astype(BF16)

    theirs = pl.ds(pl.multiple_of((1 - core) * own_rows, own_rows), own_rows)
    mine = pl.ds(pl.multiple_of(core * own_rows, own_rows), own_rows)
    last_copies = []
    for step in range(steps):
        lanes = slice(step * chunk, (step + 1) * chunk)
        tail[:, lanes] = dot(context[...], po_v[:, lanes])
        last_out[step] = tail[theirs, lanes].astype(BF16)
        last_copies.append(
            pltpu.make_async_remote_copy(
                src_ref=last_out.at[step], dst_ref=last_in.at[step],
                send_sem=last_send.at[step], recv_sem=last_recv.at[step],
                device_id=twin, device_id_type=MESH,
            )
        )
        last_copies[-1].start()
    for step in range(steps):
        lanes = slice(step * chunk, (step + 1) * chunk)
        part = hidden[mine, lanes] + tail[mine, lanes]
        last_copies[step].wait()
        out[:, lanes] = (part + last_in[step].astype(F32)).astype(BF16)


def local(*args):
    args = args[:12] + (args[12].T, args[13].T)
    fields, mesh_state = args[0], args[1]
    send_rows = args[11]
    ch, half = fields.shape
    nodes, width = mesh_state.shape
    cols = args[3].shape[1]
    pairs = cols // LANES
    remote = send_rows.shape[1] * send_rows.shape[2]
    columns = 2 * half + remote
    copies = [pltpu.VMEM(x.shape, x.dtype) for x in args]
    buffers = [
        pltpu.VMEM((ch, half), BF16),
        pltpu.VMEM((remote, LANES), BF16),
        pltpu.VMEM((2, remote, LANES), BF16),
        pltpu.VMEM((2 * LANES, 2 * half), BF16),
        pltpu.VMEM((2 * half, LANES), BF16),
        pltpu.VMEM((2 * half, cols), BF16),
        pltpu.VMEM((nodes, columns), F32),
        pltpu.VMEM((pairs, 2 * nodes, 2 * LANES), BF16),
        pltpu.VMEM((nodes, width), F32),
        pltpu.VMEM((STEPS, nodes, width // STEPS), BF16),
        pltpu.VMEM((STEPS, nodes, width // STEPS), BF16),
        pltpu.VMEM((nodes, cols), BF16),
        pltpu.VMEM((nodes, width), F32),
        pltpu.VMEM((STEPS, nodes // 2, width // STEPS), BF16),
        pltpu.VMEM((STEPS, nodes // 2, width // STEPS), BF16),
    ]
    semaphores = [
        pltpu.SemaphoreType.DMA((len(args),)),
        pltpu.SemaphoreType.DMA((2,)),
        pltpu.SemaphoreType.DMA((2 * NEIGH,)),
        pltpu.SemaphoreType.DMA((2 * NEIGH,)),
    ] + [pltpu.SemaphoreType.DMA((STEPS,))] * 4 + [pltpu.SemaphoreType.REGULAR]
    return pl.pallas_call(
        kernel,
        out_shape=jax.ShapeDtypeStruct((nodes // 2, width), BF16),
        in_specs=[pl.BlockSpec(memory_space=pltpu.HBM)] * len(args),
        out_specs=pl.BlockSpec(memory_space=pltpu.VMEM),
        scratch_shapes=copies + buffers + semaphores,
        compiler_params=pltpu.CompilerParams(
            collective_id=0, has_side_effects=True, vmem_limit_bytes=56 * 1024 * 1024
        ),
        cost_estimate=pl.CostEstimate(
            flops=3_000_000_000, bytes_accessed=9_500_000, transcendentals=800_000
        ),
        name="encode_and_process",
    )(*args)


def solution(mesh):
    return jax.shard_map(
        local,
        mesh=mesh,
        in_specs=(
            P(None, ("nodes", "heads")),
            P("nodes", None),
            P(),
            P(None, "heads"),
            P(None, "heads"),
            P(None, "heads"),
            P("heads", None),
            P(None, "heads"),
            P(None, "heads"),
            P(None, "heads"),
            P("heads", None),
            P("nodes", None, None),
            P("nodes", None),
            P("nodes", None),
        ),
        out_specs=P(("nodes", "heads"), None),
        check_vma=False,
    )
```

```python
import functools
import math

import jax
import jax.numpy as jnp
from jax import lax
from jax.experimental import pallas as pl
from jax.experimental.pallas import tpu as pltpu
from jax.sharding import PartitionSpec as P

HEADS = 16
HS = 64
NEIGH = 4
STEPS = 2
F32 = jnp.float32
BF16 = jnp.bfloat16
MESH = pl.DeviceIdType.MESH
LANES = 128
LOG2E = math.log2(math.e)
NN = (((1,), (0,)), ((), ()))
NT = (((1,), (1,)), ((), ()))


def offset_of(slot):
    return (slot // 2 + 1) * (1 if slot % 2 == 0 else -1)


def dot(a, b, dims=NN):
    return lax.dot_general(a, b, dims, preferred_element_type=F32)


def split(x):
    high = x.astype(BF16)
    return high, (x - high.astype(F32)).astype(BF16)


def normalize(x):
    centred = x - jnp.mean(x, axis=-1, keepdims=True)
    spread = jnp.mean(centred * centred, axis=-1, keepdims=True)
    return centred * lax.rsqrt(spread + 1e-05)


def iota(shape, axis):
    return lax.broadcasted_iota(jnp.int32, shape, axis)


def kernel(
    fields, mesh_state, w_embed, w_q, w_k, w_v, w_o, p_q, p_k, p_v, p_o, send_rows, senders, mask,
    out,
    own_v, mesh_v, embed_v, wq_v, wk_v, wv_v, wo_v, pq_v, pk_v, pv_v, po_v, rows_v, send_v, mask_v,
    other_v, listed, received, table, last, values, bias, queries, hidden, sums_out, sums_in,
    context, tail, last_out, last_in,
    load_sem, half_sem, list_send, list_recv, sum_send, sum_recv, last_send, last_recv,
    wrap_sem,
):
    n = lax.axis_size("nodes")
    region, core = lax.axis_index("nodes"), lax.axis_index("heads")
    twin = {"nodes": region, "heads": 1 - core}
    ch, half = fields.shape
    nodes, width = mesh_state.shape
    fan = senders.shape[0]
    cols = w_q.shape[1]
    pairs = cols // LANES
    cap = send_rows.shape[2]
    points = 2 * half
    remote = NEIGH * cap
    own_rows = nodes // 2
    steps = sums_out.shape[0]
    chunk = width // steps
    exponent = LOG2E / math.sqrt(HS)

    def neighbour(slot, other):
        place = lax.rem(region + (offset_of(slot) + n), n)
        return {"nodes": place, "heads": 1 - core if other else core}

    loads = {}
    pieces = [
        (fields, own_v), (send_rows, rows_v), (w_embed, embed_v), (senders, send_v), (mask, mask_v),
        (mesh_state, mesh_v), (w_q, wq_v), (w_k, wk_v), (w_v, wv_v), (w_o, wo_v),
        (p_q, pq_v), (p_k, pk_v), (p_v, pv_v), (p_o, po_v),
    ]
    for index, (source, target) in enumerate(pieces):
        loads[id(target)] = pltpu.make_async_copy(source, target, load_sem.at[index])

    def loaded(*targets):
        for target in targets:
            loads.pop(id(target)).wait()

    for _, target in pieces[:3]:
        loads[id(target)].start()
    barrier = pltpu.get_barrier_semaphore()

    def greet(slot, semaphore):
        for other in range(2):
            pl.semaphore_signal(
                semaphore, inc=1, device_id=neighbour(slot, other), device_id_type=MESH
            )

    pl.semaphore_signal(barrier, inc=1, device_id=twin, device_id_type=MESH)
    for slot in range(NEIGH):
        if offset_of(slot) < 0:
            greet(slot, barrier)
        else:
            pl.when(region + offset_of(slot) < n)(functools.partial(greet, slot, barrier))
    late = sum((region + offset_of(slot) < 0).astype(jnp.int32) for slot in range(NEIGH))
    for _, target in pieces[3:]:
        loads[id(target)].start()

    loaded(own_v, rows_v)
    widen = (iota((LANES, ch), 0) == iota((LANES, ch), 1)).astype(BF16)
    own = dot(widen, own_v[...]).astype(BF16)
    rows = rows_v[0]
    wanted = jnp.concatenate([rows[j : j + 1, :] for j in range(NEIGH)], axis=1) - core * half
    pick = (iota((half, remote), 0) == wanted).astype(BF16)
    listed[...] = dot(own, pick).T.astype(BF16)

    pl.semaphore_wait(barrier, 1 + 2 * NEIGH - 2 * late)
    def list_copies(slot):
        part = pl.ds(slot * cap, cap)
        return [
            pltpu.make_async_remote_copy(
                src_ref=listed.at[part], dst_ref=received.at[other, part],
                send_sem=list_send.at[2 * slot + other], recv_sem=list_recv.at[2 * slot + other],
                device_id=neighbour(slot, other), device_id_type=MESH,
            )
            for other in range(2)
        ]

    def send_list(slot):
        for copy in list_copies(slot):
            copy.start()

    ahead = [slot for slot in range(NEIGH) if offset_of(slot) > 0]
    behind = [slot for slot in range(NEIGH) if offset_of(slot) < 0]
    for slot in ahead:
        send_list(slot)
    for slot in ahead:
        pl.when(region + offset_of(slot) >= n)(functools.partial(greet, slot, wrap_sem))
    for slot in behind:
        pl.when(region + offset_of(slot) >= 0)(functools.partial(send_list, slot))
    half_copy = pltpu.make_async_remote_copy(
        src_ref=fields, dst_ref=other_v, send_sem=half_sem.at[0], recv_sem=half_sem.at[1],
        device_id=twin, device_id_type=MESH,
    )
    half_copy.start()

    loaded(embed_v)
    embed = dot(widen, embed_v[...])
    embed = jnp.where(iota((LANES, 1), 0) == ch, 1.0, embed).astype(BF16)
    gram = dot(embed, embed, NT) * (1.0 / width)
    mean = gram[:, ch : ch + 1]
    gram = jnp.concatenate(split(gram - mean * gram[ch : ch + 1, :]), axis=1)

    def through(weight):
        both = dot(embed, weight[...])
        return split(both - mean * both[ch : ch + 1, :])

    def inverse_of(squares, axis):
        squares = jnp.maximum(jnp.sum(squares, axis=axis, keepdims=True), 0.0)
        return lax.rsqrt(squares + 1e-05)

    def place_half(block, first):
        twice = jnp.concatenate([block, block], axis=0)
        table[:, first : first + half] = twice
        block = block.astype(F32)
        squares = dot(gram, twice) * block
        last[first : first + half, :] = block.T.astype(BF16)
        return inverse_of(squares, 0), inverse_of(squares.T, 1)

    inverse, scale = place_half(own, 0)

    loaded(send_v, mask_v)
    spot = send_v[...]
    tiles = (points + remote) // LANES
    word = jnp.zeros_like(spot)
    for tile in range(tiles):
        word = jnp.where(spot >= tile * LANES, 1 << (6 * tile), word)
    word = jnp.where(mask_v[...] > 0, word, 0)
    spot = spot & (LANES - 1)
    down = iota((LANES, nodes), 0)
    counts = jnp.zeros((LANES, nodes), jnp.int32)
    for slot in range(fan):
        counts += jnp.where(spot[slot : slot + 1, :] == down, word[slot : slot + 1, :], 0)
    counts = counts.T
    for tile in range(tiles):
        total = ((counts >> (6 * tile)) & 63).astype(F32)
        total = jnp.where(total > 0, jnp.log2(jnp.maximum(total, 1.0)), -1e30)
        first = tile * LANES
        if first < points:
            first = lax.rem(first + core * half, points)
        bias[:, pl.ds(pl.multiple_of(first, LANES), LANES)] = total

    loaded(mesh_v, wq_v)
    normed = normalize(mesh_v[...].astype(F32)).astype(BF16)
    enc_queries = dot(normed, wq_v[...]).astype(BF16)

    loaded(wk_v)
    k_high, k_low = through(wk_v)
    low_lanes = iota((nodes, LANES), 1) < HS

    def lanes_of(pair):
        return slice(pair * LANES, (pair + 1) * LANES)

    def rows_of(pair):
        return slice(2 * pair * nodes, 2 * (pair + 1) * nodes)

    def two_heads(rows):
        zeros = jnp.zeros_like(rows)
        even, odd = jnp.where(low_lanes, rows, zeros), jnp.where(low_lanes, zeros, rows)
        return jnp.concatenate([even, odd], axis=0)

    for pair in range(pairs):
        lanes = lanes_of(pair)
        two = two_heads(enc_queries[:, lanes])
        keys = jnp.concatenate([k_high[:, lanes], k_low[:, lanes]], axis=1)
        high, low = split(dot(jnp.concatenate([two, two], axis=1), keys, NT))
        queries[rows_of(pair), 0:LANES] = high
        queries[rows_of(pair), LANES : 2 * LANES] = low

    loaded(wv_v)
    v_both = jnp.concatenate(through(wv_v), axis=0)

    def values_of(rows, scale):
        return (dot(jnp.concatenate([rows, rows], axis=1), v_both) * scale).astype(BF16)

    def weigh(logits, edges, inverse):
        logits = logits * (inverse * exponent) + jnp.concatenate([edges, edges], axis=0)
        top = jnp.max(logits, axis=-1, keepdims=True)
        return top, jnp.exp2(logits - top).astype(BF16)

    def join_heads(rows):
        return jnp.where(low_lanes, rows[:nodes], rows[nodes:])

    def mix(probs, values):
        mixed = dot(probs, jnp.concatenate([values, jnp.ones_like(values)], axis=1))
        return join_heads(mixed[:, :LANES]), join_heads(mixed[:, LANES:])

    half_copy.wait_recv()
    other_inverse, other_scale = place_half(dot(widen, other_v[...]).astype(BF16), half)
    inverse = jnp.concatenate([inverse, other_inverse], axis=1)
    values[0:half, :] = values_of(last[0:half, :], scale)
    values[half:points, :] = values_of(last[half:points, :], other_scale)
    near = []
    for pair in range(pairs):
        logits = dot(queries[rows_of(pair), :], table[...])
        top, probs = weigh(logits, bias[:, 0:points], inverse)
        near.append((join_heads(top), *mix(probs, values[:, lanes_of(pair)])))

    loaded(wo_v)
    pl.when(late > 0)(lambda: pl.semaphore_wait(wrap_sem, 2 * late))
    for slot in behind:
        pl.when(region + offset_of(slot) < 0)(functools.partial(send_list, slot))
    for slot in range(NEIGH):
        for copy in list_copies(slot):
            copy.wait_recv()
    far = received[0] + received[1]
    far_twice = jnp.concatenate([far, far], axis=1)
    squares = dot(far_twice, gram, NT) * far.astype(F32)
    inverse = inverse_of(squares.T, 0)
    far_down = far.astype(F32).T.astype(BF16)
    far_down = jnp.concatenate([far_down, far_down], axis=0)
    middle = pairs * nodes
    far_logits = jnp.concatenate(
        [dot(queries[0:middle, :], far_down), dot(queries[middle : 2 * middle, :], far_down)], axis=0
    )
    far_weights = [
        weigh(far_logits[rows_of(pair)], bias[:, points : points + remote], inverse)
        for pair in range(pairs)
    ]
    far_values = values_of(far, inverse_of(squares, 1))
    for pair in range(pairs):
        lanes = lanes_of(pair)
        top, probs = far_weights[pair]
        mixed, total = mix(probs, far_values[:, lanes])
        near_top, near_mixed, near_total = near[pair]
        top = join_heads(top)
        best = jnp.maximum(top, near_top)
        gain, near_gain = jnp.exp2(top - best), jnp.exp2(near_top - best)
        both = gain * mixed + near_gain * near_mixed
        context[:, lanes] = (both / (gain * total + near_gain * near_total)).astype(BF16)

    sum_copies = []
    for step in range(steps):
        lanes = slice(step * chunk, (step + 1) * chunk)
        part = dot(context[...], wo_v[:, lanes])
        sums_out[step] = part.astype(BF16)
        sum_copies.append(
            pltpu.make_async_remote_copy(
                src_ref=sums_out.at[step], dst_ref=sums_in.at[step],
                send_sem=sum_send.at[step], recv_sem=sum_recv.at[step],
                device_id=twin, device_id_type=MESH,
            )
        )
        sum_copies[-1].start()
        hidden[:, lanes] = mesh_v[:, lanes].astype(F32) + part
    loaded(pq_v, pk_v, pv_v, po_v)
    for step in range(steps):
        lanes = slice(step * chunk, (step + 1) * chunk)
        sum_copies[step].wait_recv()
        hidden[:, lanes] += sums_in[step].astype(F32)

    normed = normalize(hidden[...]).astype(BF16)
    proc_q = dot(normed, pq_v[...]).astype(BF16)
    proc_k = dot(normed, pk_v[...]).astype(BF16)
    probs = []
    for pair in range(pairs):
        lanes = lanes_of(pair)
        logits = dot(two_heads(proc_q[:, lanes]), proc_k[:, lanes], NT) * exponent
        probs.append(jnp.exp2(logits - jnp.max(logits, axis=-1, keepdims=True)).astype(BF16))
    proc_v = dot(normed, pv_v[...]).astype(BF16)
    for pair in range(pairs):
        lanes = lanes_of(pair)
        mixed, total = mix(probs[pair], proc_v[:, lanes])
        context[:, lanes] = (mixed / total).astype(BF16)

    theirs = pl.ds(pl.multiple_of((1 - core) * own_rows, own_rows), own_rows)
    mine = pl.ds(pl.multiple_of(core * own_rows, own_rows), own_rows)
    last_copies = []
    for step in range(steps):
        lanes = slice(step * chunk, (step + 1) * chunk)
        tail[:, lanes] = dot(context[...], po_v[:, lanes])
        last_out[step] = tail[theirs, lanes].astype(BF16)
        last_copies.append(
            pltpu.make_async_remote_copy(
                src_ref=last_out.at[step], dst_ref=last_in.at[step],
                send_sem=last_send.at[step], recv_sem=last_recv.at[step],
                device_id=twin, device_id_type=MESH,
            )
        )
        last_copies[-1].start()
    for step in range(steps):
        lanes = slice(step * chunk, (step + 1) * chunk)
        part = hidden[mine, lanes] + tail[mine, lanes]
        last_copies[step].wait_recv()
        out[:, lanes] = (part + last_in[step].astype(F32)).astype(BF16)
    for copy in [half_copy, *sum_copies, *last_copies]:
        copy.wait_send()
    for slot in range(NEIGH):
        for copy in list_copies(slot):
            copy.wait_send()


def local(*args):
    args = args[:12] + (args[12].T, args[13].T)
    fields, mesh_state = args[0], args[1]
    send_rows = args[11]
    ch, half = fields.shape
    nodes, width = mesh_state.shape
    cols = args[3].shape[1]
    pairs = cols // LANES
    remote = send_rows.shape[1] * send_rows.shape[2]
    columns = 2 * half + remote
    copies = [pltpu.VMEM(x.shape, x.dtype) for x in args]
    buffers = [
        pltpu.VMEM((ch, half), BF16),
        pltpu.VMEM((remote, LANES), BF16),
        pltpu.VMEM((2, remote, LANES), BF16),
        pltpu.VMEM((2 * LANES, 2 * half), BF16),
        pltpu.VMEM((2 * half, LANES), BF16),
        pltpu.VMEM((2 * half, cols), BF16),
        pltpu.VMEM((nodes, columns), F32),
        pltpu.VMEM((pairs * 2 * nodes, 2 * LANES), BF16),
        pltpu.VMEM((nodes, width), F32),
        pltpu.VMEM((STEPS, nodes, width // STEPS), BF16),
        pltpu.VMEM((STEPS, nodes, width // STEPS), BF16),
        pltpu.VMEM((nodes, cols), BF16),
        pltpu.VMEM((nodes, width), F32),
        pltpu.VMEM((STEPS, nodes // 2, width // STEPS), BF16),
        pltpu.VMEM((STEPS, nodes // 2, width // STEPS), BF16),
    ]
    semaphores = [
        pltpu.SemaphoreType.DMA((len(args),)),
        pltpu.SemaphoreType.DMA((2,)),
        pltpu.SemaphoreType.DMA((2 * NEIGH,)),
        pltpu.SemaphoreType.DMA((2 * NEIGH,)),
    ] + [pltpu.SemaphoreType.DMA((STEPS,))] * 4 + [pltpu.SemaphoreType.REGULAR]
    return pl.pallas_call(
        kernel,
        out_shape=pltpu.VMEM((nodes // 2, width), BF16),
        in_specs=[pl.BlockSpec(memory_space=pltpu.HBM)] * len(args),
        out_specs=pl.BlockSpec(memory_space=pltpu.VMEM),
        scratch_shapes=copies + buffers + semaphores,
        compiler_params=pltpu.CompilerParams(
            collective_id=0, has_side_effects=True, vmem_limit_bytes=56 * 1024 * 1024
        ),
        cost_estimate=pl.CostEstimate(
            flops=3_000_000_000, bytes_accessed=9_500_000, transcendentals=800_000
        ),
        name="encode_and_process",
    )(*args)


def solution(mesh):
    return jax.shard_map(
        local,
        mesh=mesh,
        in_specs=(
            P(None, ("nodes", "heads")),
            P("nodes", None),
            P(),
            P(None, "heads"),
            P(None, "heads"),
            P(None, "heads"),
            P("heads", None),
            P(None, "heads"),
            P(None, "heads"),
            P(None, "heads"),
            P("heads", None),
            P("nodes", None, None),
            P("nodes", None),
            P("nodes", None),
        ),
        out_specs=P(("nodes", "heads"), None),
        check_vma=False,
    )
```

```python
import functools
import math

import jax
import jax.numpy as jnp
from jax import lax
from jax.experimental import pallas as pl
from jax.experimental.pallas import tpu as pltpu
from jax.sharding import PartitionSpec as P

HEADS = 16
HS = 64
NEIGH = 4
STEPS = 2
F32 = jnp.float32
BF16 = jnp.bfloat16
MESH = pl.DeviceIdType.MESH
LANES = 128
LOG2E = math.log2(math.e)
NN = (((1,), (0,)), ((), ()))
NT = (((1,), (1,)), ((), ()))


def offset_of(slot):
    return (slot // 2 + 1) * (1 if slot % 2 == 0 else -1)


def dot(a, b, dims=NN):
    return lax.dot_general(a, b, dims, preferred_element_type=F32)


def split(x):
    high = x.astype(BF16)
    return high, (x - high.astype(F32)).astype(BF16)


def normalize(x):
    centred = x - jnp.mean(x, axis=-1, keepdims=True)
    spread = jnp.mean(centred * centred, axis=-1, keepdims=True)
    return centred * lax.rsqrt(spread + 1e-05)


def iota(shape, axis):
    return lax.broadcasted_iota(jnp.int32, shape, axis)


def kernel(
    fields, mesh_state, w_embed, w_q, w_k, w_v, w_o, p_q, p_k, p_v, p_o, send_rows, senders, mask,
    out,
    own_v, mesh_v, embed_v, wq_v, wk_v, wv_v, wo_v, pq_v, pk_v, pv_v, po_v, rows_v, send_v, mask_v,
    other_v, listed, received, table, last, values, bias, queries, hidden,     context, tail, last_out, last_in, w_other, w_joint, context_in, ahead_sum,
    context_late,
    load_sem, half_sem, list_send, list_recv, weight_sem, sum_send, sum_recv, last_send, last_recv,
    wrap_sem,
):
    n = lax.axis_size("nodes")
    region, core = lax.axis_index("nodes"), lax.axis_index("heads")
    twin = {"nodes": region, "heads": 1 - core}
    ch, half = fields.shape
    nodes, width = mesh_state.shape
    fan = senders.shape[0]
    cols = w_q.shape[1]
    pairs = cols // LANES
    cap = send_rows.shape[2]
    points = 2 * half
    remote = NEIGH * cap
    own_rows = nodes // 2
    steps = last_out.shape[0]
    chunk = width // steps
    exponent = LOG2E / math.sqrt(HS)

    def neighbour(slot, other):
        place = lax.rem(region + (offset_of(slot) + n), n)
        return {"nodes": place, "heads": 1 - core if other else core}

    loads = {}
    pieces = [
        (fields, own_v), (send_rows, rows_v), (w_embed, embed_v), (senders, send_v), (mask, mask_v),
        (mesh_state, mesh_v), (w_q, wq_v), (w_k, wk_v), (w_v, wv_v), (w_o, wo_v),
        (p_q, pq_v), (p_k, pk_v), (p_v, pv_v), (p_o, po_v),
    ]
    for index, (source, target) in enumerate(pieces):
        loads[id(target)] = pltpu.make_async_copy(source, target, load_sem.at[index])

    def loaded(*targets):
        for target in targets:
            loads.pop(id(target)).wait()

    for _, target in pieces[:3]:
        loads[id(target)].start()
    barrier = pltpu.get_barrier_semaphore()

    def greet(slot, semaphore):
        for other in range(2):
            pl.semaphore_signal(
                semaphore, inc=1, device_id=neighbour(slot, other), device_id_type=MESH
            )

    pl.semaphore_signal(barrier, inc=1, device_id=twin, device_id_type=MESH)
    for slot in range(NEIGH):
        if offset_of(slot) < 0:
            greet(slot, barrier)
        else:
            pl.when(region + offset_of(slot) < n)(functools.partial(greet, slot, barrier))
    late = sum((region + offset_of(slot) < 0).astype(jnp.int32) for slot in range(NEIGH))
    for _, target in pieces[3:]:
        loads[id(target)].start()

    loaded(own_v, rows_v)
    widen = (iota((LANES, ch), 0) == iota((LANES, ch), 1)).astype(BF16)
    own = dot(widen, own_v[...]).astype(BF16)
    rows = rows_v[0]
    wanted = jnp.concatenate([rows[j : j + 1, :] for j in range(NEIGH)], axis=1) - core * half
    pick = (iota((half, remote), 0) == wanted).astype(BF16)
    listed[...] = dot(own, pick).T.astype(BF16)

    pl.semaphore_wait(barrier, 1 + 2 * NEIGH - 2 * late)
    def list_copies(slot):
        part = pl.ds(slot * cap, cap)
        return [
            pltpu.make_async_remote_copy(
                src_ref=listed.at[part], dst_ref=received.at[other, part],
                send_sem=list_send.at[2 * slot + other], recv_sem=list_recv.at[2 * slot + other],
                device_id=neighbour(slot, other), device_id_type=MESH,
            )
            for other in range(2)
        ]

    def send_list(slot):
        for copy in list_copies(slot):
            copy.start()

    ahead = [slot for slot in range(NEIGH) if offset_of(slot) > 0]
    behind = [slot for slot in range(NEIGH) if offset_of(slot) < 0]
    for slot in ahead:
        send_list(slot)
    for slot in ahead:
        pl.when(region + offset_of(slot) >= n)(functools.partial(greet, slot, wrap_sem))
    for slot in behind:
        pl.when(region + offset_of(slot) >= 0)(functools.partial(send_list, slot))
    half_copy = pltpu.make_async_remote_copy(
        src_ref=fields, dst_ref=other_v, send_sem=half_sem.at[0], recv_sem=half_sem.at[1],
        device_id=twin, device_id_type=MESH,
    )
    half_copy.start()
    weight_copy = pltpu.make_async_remote_copy(
        src_ref=w_o, dst_ref=w_other, send_sem=weight_sem.at[0], recv_sem=weight_sem.at[1],
        device_id=twin, device_id_type=MESH,
    )
    weight_copy.start()

    loaded(embed_v)
    embed = dot(widen, embed_v[...])
    embed = jnp.where(iota((LANES, 1), 0) == ch, 1.0, embed).astype(BF16)
    gram = dot(embed, embed, NT) * (1.0 / width)
    mean = gram[:, ch : ch + 1]
    gram = split(gram - mean * gram[ch : ch + 1, :])
    gram_down = jnp.concatenate(gram, axis=0)
    gram = jnp.concatenate(gram, axis=1)

    def through(weight):
        both = dot(embed, weight[...])
        return split(both - mean * both[ch : ch + 1, :])

    def inverse_of(squares, axis):
        squares = jnp.maximum(jnp.sum(squares, axis=axis, keepdims=True), 0.0)
        return lax.rsqrt(squares + 1e-05)

    def place_half(block, first):
        twice = jnp.concatenate([block, block], axis=0)
        table[:, first : first + half] = twice
        block = block.astype(F32)
        squares = dot(gram, twice) * block
        last[first : first + half, :] = block.T.astype(BF16)
        return inverse_of(squares, 0), inverse_of(squares.T, 1)

    inverse, scale = place_half(own, 0)

    loaded(send_v, mask_v)
    spot = send_v[...]
    tiles = (points + remote) // LANES
    word = jnp.zeros_like(spot)
    for tile in range(tiles):
        word = jnp.where(spot >= tile * LANES, 1 << (6 * tile), word)
    word = jnp.where(mask_v[...] > 0, word, 0)
    spot = spot & (LANES - 1)
    down = iota((LANES, nodes), 0)
    counts = jnp.zeros((LANES, nodes), jnp.int32)
    for slot in range(fan):
        counts += jnp.where(spot[slot : slot + 1, :] == down, word[slot : slot + 1, :], 0)
    counts = counts.T
    for tile in range(tiles):
        total = ((counts >> (6 * tile)) & 63).astype(F32)
        total = jnp.where(total > 0, jnp.log2(jnp.maximum(total, 1.0)), -1e30)
        first = tile * LANES
        if first < points:
            first = lax.rem(first + core * half, points)
        bias[:, pl.ds(pl.multiple_of(first, LANES), LANES)] = total

    loaded(mesh_v, wq_v)
    normed = normalize(mesh_v[...].astype(F32)).astype(BF16)
    enc_queries = dot(normed, wq_v[...]).astype(BF16)

    loaded(wk_v)
    k_high, k_low = through(wk_v)
    low_lanes = iota((nodes, LANES), 1) < HS

    def lanes_of(pair):
        return slice(pair * LANES, (pair + 1) * LANES)

    def rows_of(pair):
        return slice(2 * pair * nodes, 2 * (pair + 1) * nodes)

    def two_heads(rows):
        zeros = jnp.zeros_like(rows)
        even, odd = jnp.where(low_lanes, rows, zeros), jnp.where(low_lanes, zeros, rows)
        return jnp.concatenate([even, odd], axis=0)

    for pair in range(pairs):
        lanes = lanes_of(pair)
        two = two_heads(enc_queries[:, lanes])
        keys = jnp.concatenate([k_high[:, lanes], k_low[:, lanes]], axis=1)
        high, low = split(dot(jnp.concatenate([two, two], axis=1), keys, NT))
        queries[rows_of(pair), 0:LANES] = high
        queries[rows_of(pair), LANES : 2 * LANES] = low

    loaded(wv_v)
    v_both = jnp.concatenate(through(wv_v), axis=0)

    def values_of(rows, scale):
        return (dot(jnp.concatenate([rows, rows], axis=1), v_both) * scale).astype(BF16)

    def weigh(logits, edges, inverse):
        logits = logits * (inverse * exponent) + jnp.concatenate([edges, edges], axis=0)
        top = jnp.max(logits, axis=-1, keepdims=True)
        return top, jnp.exp2(logits - top).astype(BF16)

    def join_heads(rows):
        return jnp.where(low_lanes, rows[:nodes], rows[nodes:])

    def mix(probs, values):
        mixed = dot(probs, jnp.concatenate([values, jnp.ones_like(values)], axis=1))
        return join_heads(mixed[:, :LANES]), join_heads(mixed[:, LANES:])

    half_copy.wait_recv()
    other_inverse, other_scale = place_half(dot(widen, other_v[...]).astype(BF16), half)
    inverse = jnp.concatenate([inverse, other_inverse], axis=1)
    values[0:half, :] = values_of(last[0:half, :], scale)
    values[half:points, :] = values_of(last[half:points, :], other_scale)
    near = []
    for pair in range(pairs):
        logits = dot(queries[rows_of(pair), :], table[...])
        top, probs = weigh(logits, bias[:, 0:points], inverse)
        near.append((join_heads(top), *mix(probs, values[:, lanes_of(pair)])))

    loaded(pq_v, pk_v, pv_v, po_v)
    weight_copy.wait_recv()
    processor = (pq_v, pk_v, pv_v)
    sums = []
    for index, weight in enumerate(processor):
        w_joint[index] = dot(w_other[...], weight[...]).astype(BF16)
        sums.append(dot(jnp.ones((8, width), BF16), weight[...])[0:1])

    loaded(wo_v)
    pl.when(late > 0)(lambda: pl.semaphore_wait(wrap_sem, 2 * late))
    for slot in behind:
        pl.when(region + offset_of(slot) < 0)(functools.partial(send_list, slot))
    for slot in range(NEIGH):
        for copy in list_copies(slot):
            copy.wait_recv()
    far = received[0] + received[1]
    far_twice = jnp.concatenate([far, far], axis=1)
    squares = dot(far_twice, gram_down) * far.astype(F32)
    inverse = inverse_of(squares.T, 0)
    middle = pairs * nodes
    far_logits = jnp.concatenate(
        [dot(queries[0:middle, :], far_twice, NT), dot(queries[middle:, :], far_twice, NT)], axis=0
    )
    far_weights = [
        weigh(far_logits[rows_of(pair)], bias[:, points : points + remote], inverse)
        for pair in range(pairs)
    ]
    far_values = values_of(far, inverse_of(squares, 1))
    for pair in range(pairs):
        lanes = lanes_of(pair)
        top, probs = far_weights[pair]
        mixed, total = mix(probs, far_values[:, lanes])
        near_top, near_mixed, near_total = near[pair]
        top = join_heads(top)
        best = jnp.maximum(top, near_top)
        gain, near_gain = jnp.exp2(top - best), jnp.exp2(near_top - best)
        both = gain * mixed + near_gain * near_mixed
        context[:, lanes] = (both / (gain * total + near_gain * near_total)).astype(BF16)

    sum_copy = pltpu.make_async_remote_copy(
        src_ref=context, dst_ref=context_in, send_sem=sum_send.at[0], recv_sem=sum_recv.at[0],
        device_id=twin, device_id_type=MESH,
    )
    sum_copy.start()
    start = mesh_v[...].astype(F32) + dot(context[...], wo_v[...])
    shift = jnp.mean(start, axis=-1, keepdims=True)
    start = start - shift
    hidden[...] = start
    start = start.astype(BF16)
    for index, weight in enumerate(processor):
        ahead_sum[index] = dot(start, weight[...])
    sum_copy.wait_recv()

    theirs_in = context_in[...]
    centred = hidden[...] + dot(theirs_in, w_other[...])
    mean = jnp.mean(centred, axis=-1, keepdims=True)
    hidden[...] = centred + shift
    spread = jnp.mean(centred * centred, axis=-1, keepdims=True) - mean * mean
    rise = lax.rsqrt(jnp.maximum(spread, 0.0) + 1e-05)

    raw = [ahead_sum[index] + dot(theirs_in, w_joint[index]) for index in range(3)]

    def projected(index):
        return ((raw[index] - mean * sums[index]) * rise).astype(BF16)

    proc_q, proc_k = projected(0), projected(1)
    probs = []
    for pair in range(pairs):
        lanes = lanes_of(pair)
        logits = dot(two_heads(proc_q[:, lanes]), proc_k[:, lanes], NT) * exponent
        probs.append(jnp.exp2(logits - jnp.max(logits, axis=-1, keepdims=True)).astype(BF16))
    proc_v = projected(2)
    for pair in range(pairs):
        lanes = lanes_of(pair)
        mixed, total = mix(probs[pair], proc_v[:, lanes])
        context_late[:, lanes] = (mixed / total).astype(BF16)

    theirs = pl.ds(pl.multiple_of((1 - core) * own_rows, own_rows), own_rows)
    mine = pl.ds(pl.multiple_of(core * own_rows, own_rows), own_rows)
    last_copies = []
    for step in range(steps):
        lanes = slice(step * chunk, (step + 1) * chunk)
        tail[:, lanes] = dot(context_late[...], po_v[:, lanes])
        last_out[step] = tail[theirs, lanes].astype(BF16)
        last_copies.append(
            pltpu.make_async_remote_copy(
                src_ref=last_out.at[step], dst_ref=last_in.at[step],
                send_sem=last_send.at[step], recv_sem=last_recv.at[step],
                device_id=twin, device_id_type=MESH,
            )
        )
        last_copies[-1].start()
    for step in range(steps):
        lanes = slice(step * chunk, (step + 1) * chunk)
        part = hidden[mine, lanes] + tail[mine, lanes]
        last_copies[step].wait_recv()
        out[:, lanes] = (part + last_in[step].astype(F32)).astype(BF16)
    for copy in [half_copy, weight_copy, sum_copy, *last_copies]:
        copy.wait_send()
    for slot in range(NEIGH):
        for copy in list_copies(slot):
            copy.wait_send()


def local(*args):
    args = args[:12] + (args[12].T, args[13].T)
    fields, mesh_state = args[0], args[1]
    send_rows = args[11]
    ch, half = fields.shape
    nodes, width = mesh_state.shape
    cols = args[3].shape[1]
    pairs = cols // LANES
    remote = send_rows.shape[1] * send_rows.shape[2]
    columns = 2 * half + remote
    copies = [pltpu.VMEM(x.shape, x.dtype) for x in args]
    buffers = [
        pltpu.VMEM((ch, half), BF16),
        pltpu.VMEM((remote, LANES), BF16),
        pltpu.VMEM((2, remote, LANES), BF16),
        pltpu.VMEM((2 * LANES, 2 * half), BF16),
        pltpu.VMEM((2 * half, LANES), BF16),
        pltpu.VMEM((2 * half, cols), BF16),
        pltpu.VMEM((nodes, columns), F32),
        pltpu.VMEM((pairs * 2 * nodes, 2 * LANES), BF16),
        pltpu.VMEM((nodes, width), F32),
        pltpu.VMEM((nodes, cols), BF16),
        pltpu.VMEM((nodes, width), F32),
        pltpu.VMEM((STEPS, nodes // 2, width // STEPS), BF16),
        pltpu.VMEM((STEPS, nodes // 2, width // STEPS), BF16),
        pltpu.VMEM((cols, width), BF16),
        pltpu.VMEM((3, cols, cols), BF16),
        pltpu.VMEM((nodes, cols), BF16),
        pltpu.VMEM((3, nodes, cols), F32),
        pltpu.VMEM((nodes, cols), BF16),
    ]
    semaphores = [
        pltpu.SemaphoreType.DMA((len(args),)),
        pltpu.SemaphoreType.DMA((2,)),
        pltpu.SemaphoreType.DMA((2 * NEIGH,)),
        pltpu.SemaphoreType.DMA((2 * NEIGH,)),
        pltpu.SemaphoreType.DMA((2,)),
        pltpu.SemaphoreType.DMA((1,)),
        pltpu.SemaphoreType.DMA((1,)),
    ] + [pltpu.SemaphoreType.DMA((STEPS,))] * 2 + [pltpu.SemaphoreType.REGULAR]
    return pl.pallas_call(
        kernel,
        out_shape=pltpu.VMEM((nodes // 2, width), BF16),
        in_specs=[pl.BlockSpec(memory_space=pltpu.HBM)] * len(args),
        out_specs=pl.BlockSpec(memory_space=pltpu.VMEM),
        scratch_shapes=copies + buffers + semaphores,
        compiler_params=pltpu.CompilerParams(
            collective_id=0, has_side_effects=True, vmem_limit_bytes=56 * 1024 * 1024
        ),
        cost_estimate=pl.CostEstimate(
            flops=3_000_000_000, bytes_accessed=9_500_000, transcendentals=800_000
        ),
        name="encode_and_process",
    )(*args)


def solution(mesh):
    return jax.shard_map(
        local,
        mesh=mesh,
        in_specs=(
            P(None, ("nodes", "heads")),
            P("nodes", None),
            P(),
            P(None, "heads"),
            P(None, "heads"),
            P(None, "heads"),
            P("heads", None),
            P(None, "heads"),
            P(None, "heads"),
            P(None, "heads"),
            P("heads", None),
            P("nodes", None, None),
            P("nodes", None),
            P("nodes", None),
        ),
        out_specs=P(("nodes", "heads"), None),
        check_vma=False,
    )
```

```python
import functools
import math

import jax
import jax.numpy as jnp
from jax import lax
from jax.experimental import pallas as pl
from jax.experimental.pallas import tpu as pltpu
from jax.sharding import PartitionSpec as P

HEADS = 16
HS = 64
NEIGH = 4
F32 = jnp.float32
BF16 = jnp.bfloat16
MESH = pl.DeviceIdType.MESH
LANES = 128
LOG2E = math.log2(math.e)
NN = (((1,), (0,)), ((), ()))
NT = (((1,), (1,)), ((), ()))


def offset_of(slot):
    return (slot // 2 + 1) * (1 if slot % 2 == 0 else -1)


def dot(a, b, dims=NN):
    return lax.dot_general(a, b, dims, preferred_element_type=F32)


def split(x):
    high = x.astype(BF16)
    return high, (x - high.astype(F32)).astype(BF16)


def normalize(x):
    centred = x - jnp.mean(x, axis=-1, keepdims=True)
    spread = jnp.mean(centred * centred, axis=-1, keepdims=True)
    return centred * lax.rsqrt(spread + 1e-05)


def iota(shape, axis):
    return lax.broadcasted_iota(jnp.int32, shape, axis)


def kernel(
    fields, mesh_state, w_embed, w_q, w_k, w_v, w_o, p_q, p_k, p_v, p_o, send_rows, senders, mask,
    out,
    own_v, mesh_v, embed_v, wq_v, wk_v, wv_v, wo_v, pq_v, pk_v, pv_v, po_v, rows_v, send_v, mask_v,
    other_v, listed, received, table, last, values, bias, queries, hidden,     context, tail, last_in, w_other, p_other, w_joint, context_in, ahead_sum,
    context_late,
    load_sem, half_sem, list_send, list_recv, weight_send, weight_recv, sum_send, sum_recv, last_sem,
    wrap_sem,
):
    n = lax.axis_size("nodes")
    region, core = lax.axis_index("nodes"), lax.axis_index("heads")
    twin = {"nodes": region, "heads": 1 - core}
    ch, half = fields.shape
    nodes, width = mesh_state.shape
    fan = senders.shape[0]
    cols = w_q.shape[1]
    pairs = cols // LANES
    cap = send_rows.shape[2]
    points = 2 * half
    remote = NEIGH * cap
    own_rows = nodes // 2
    exponent = LOG2E / math.sqrt(HS)

    def neighbour(slot, other):
        place = lax.rem(region + (offset_of(slot) + n), n)
        return {"nodes": place, "heads": 1 - core if other else core}

    loads = {}
    pieces = [
        (fields, own_v), (send_rows, rows_v), (w_embed, embed_v), (senders, send_v), (mask, mask_v),
        (mesh_state, mesh_v), (w_q, wq_v), (w_k, wk_v), (w_v, wv_v), (w_o, wo_v),
        (p_q, pq_v), (p_k, pk_v), (p_v, pv_v), (p_o, po_v),
    ]
    for index, (source, target) in enumerate(pieces):
        loads[id(target)] = pltpu.make_async_copy(source, target, load_sem.at[index])

    def loaded(*targets):
        for target in targets:
            loads.pop(id(target)).wait()

    for _, target in pieces[:3]:
        loads[id(target)].start()
    barrier = pltpu.get_barrier_semaphore()

    def greet(slot, semaphore):
        for other in range(2):
            pl.semaphore_signal(
                semaphore, inc=1, device_id=neighbour(slot, other), device_id_type=MESH
            )

    pl.semaphore_signal(barrier, inc=1, device_id=twin, device_id_type=MESH)
    for slot in range(NEIGH):
        if offset_of(slot) < 0:
            greet(slot, barrier)
        else:
            pl.when(region + offset_of(slot) < n)(functools.partial(greet, slot, barrier))
    late = sum((region + offset_of(slot) < 0).astype(jnp.int32) for slot in range(NEIGH))
    for _, target in pieces[3:]:
        loads[id(target)].start()

    loaded(own_v, rows_v)
    widen = (iota((LANES, ch), 0) == iota((LANES, ch), 1)).astype(BF16)
    own = dot(widen, own_v[...]).astype(BF16)
    rows = rows_v[0]
    wanted = jnp.concatenate([rows[j : j + 1, :] for j in range(NEIGH)], axis=1) - core * half
    pick = (iota((half, remote), 0) == wanted).astype(BF16)
    listed[...] = dot(own, pick).T.astype(BF16)

    pl.semaphore_wait(barrier, 1 + 2 * NEIGH - 2 * late)
    def list_copies(slot):
        part = pl.ds(slot * cap, cap)
        return [
            pltpu.make_async_remote_copy(
                src_ref=listed.at[part], dst_ref=received.at[other, part],
                send_sem=list_send.at[2 * slot + other], recv_sem=list_recv.at[2 * slot + other],
                device_id=neighbour(slot, other), device_id_type=MESH,
            )
            for other in range(2)
        ]

    def send_list(slot):
        for copy in list_copies(slot):
            copy.start()

    ahead = [slot for slot in range(NEIGH) if offset_of(slot) > 0]
    behind = [slot for slot in range(NEIGH) if offset_of(slot) < 0]
    for slot in ahead:
        send_list(slot)
    for slot in ahead:
        pl.when(region + offset_of(slot) >= n)(functools.partial(greet, slot, wrap_sem))
    for slot in behind:
        pl.when(region + offset_of(slot) >= 0)(functools.partial(send_list, slot))
    half_copy = pltpu.make_async_remote_copy(
        src_ref=fields, dst_ref=other_v, send_sem=half_sem.at[0], recv_sem=half_sem.at[1],
        device_id=twin, device_id_type=MESH,
    )
    half_copy.start()
    weight_copies = [
        pltpu.make_async_remote_copy(
            src_ref=source, dst_ref=target, send_sem=weight_send.at[index],
            recv_sem=weight_recv.at[index], device_id=twin, device_id_type=MESH,
        )
        for index, (source, target) in enumerate([(w_o, w_other), (p_o, p_other)])
    ]
    for copy in weight_copies:
        copy.start()

    loaded(embed_v)
    embed = dot(widen, embed_v[...])
    embed = jnp.where(iota((LANES, 1), 0) == ch, 1.0, embed).astype(BF16)
    gram = dot(embed, embed, NT) * (1.0 / width)
    mean = gram[:, ch : ch + 1]
    gram = split(gram - mean * gram[ch : ch + 1, :])
    gram_down = jnp.concatenate(gram, axis=0)
    gram = jnp.concatenate(gram, axis=1)

    def through(weight):
        both = dot(embed, weight[...])
        return split(both - mean * both[ch : ch + 1, :])

    def inverse_of(squares, axis):
        squares = jnp.maximum(jnp.sum(squares, axis=axis, keepdims=True), 0.0)
        return lax.rsqrt(squares + 1e-05)

    def place_half(block, first):
        twice = jnp.concatenate([block, block], axis=0)
        table[:, first : first + half] = twice
        block = block.astype(F32)
        squares = dot(gram, twice) * block
        last[first : first + half, :] = block.T.astype(BF16)
        return inverse_of(squares, 0), inverse_of(squares.T, 1)

    inverse, scale = place_half(own, 0)

    loaded(send_v, mask_v)
    spot = send_v[...]
    tiles = (points + remote) // LANES
    word = jnp.zeros_like(spot)
    for tile in range(tiles):
        word = jnp.where(spot >= tile * LANES, 1 << (6 * tile), word)
    word = jnp.where(mask_v[...] > 0, word, 0)
    spot = spot & (LANES - 1)
    down = iota((LANES, nodes), 0)
    counts = jnp.zeros((LANES, nodes), jnp.int32)
    for slot in range(fan):
        counts += jnp.where(spot[slot : slot + 1, :] == down, word[slot : slot + 1, :], 0)
    counts = counts.T
    for tile in range(tiles):
        total = ((counts >> (6 * tile)) & 63).astype(F32)
        total = jnp.where(total > 0, jnp.log2(jnp.maximum(total, 1.0)), -1e30)
        first = tile * LANES
        if first < points:
            first = lax.rem(first + core * half, points)
        bias[:, pl.ds(pl.multiple_of(first, LANES), LANES)] = total

    loaded(mesh_v, wq_v)
    normed = normalize(mesh_v[...].astype(F32)).astype(BF16)
    enc_queries = dot(normed, wq_v[...]).astype(BF16)

    loaded(wk_v)
    k_high, k_low = through(wk_v)
    low_lanes = iota((nodes, LANES), 1) < HS

    def lanes_of(pair):
        return slice(pair * LANES, (pair + 1) * LANES)

    def rows_of(pair):
        return slice(2 * pair * nodes, 2 * (pair + 1) * nodes)

    def two_heads(rows):
        zeros = jnp.zeros_like(rows)
        even, odd = jnp.where(low_lanes, rows, zeros), jnp.where(low_lanes, zeros, rows)
        return jnp.concatenate([even, odd], axis=0)

    for pair in range(pairs):
        lanes = lanes_of(pair)
        two = two_heads(enc_queries[:, lanes])
        keys = jnp.concatenate([k_high[:, lanes], k_low[:, lanes]], axis=1)
        high, low = split(dot(jnp.concatenate([two, two], axis=1), keys, NT))
        queries[rows_of(pair), 0:LANES] = high
        queries[rows_of(pair), LANES : 2 * LANES] = low

    loaded(wv_v)
    v_both = jnp.concatenate(through(wv_v), axis=0)

    def values_of(rows, scale):
        return (dot(jnp.concatenate([rows, rows], axis=1), v_both) * scale).astype(BF16)

    def weigh(logits, edges, inverse):
        logits = logits * (inverse * exponent) + jnp.concatenate([edges, edges], axis=0)
        top = jnp.max(logits, axis=-1, keepdims=True)
        return top, jnp.exp2(logits - top).astype(BF16)

    def join_heads(rows):
        return jnp.where(low_lanes, rows[:nodes], rows[nodes:])

    def mix(probs, values):
        mixed = dot(probs, jnp.concatenate([values, jnp.ones_like(values)], axis=1))
        return join_heads(mixed[:, :LANES]), join_heads(mixed[:, LANES:])

    half_copy.wait_recv()
    other_inverse, other_scale = place_half(dot(widen, other_v[...]).astype(BF16), half)
    inverse = jnp.concatenate([inverse, other_inverse], axis=1)
    values[0:half, :] = values_of(last[0:half, :], scale)
    values[half:points, :] = values_of(last[half:points, :], other_scale)
    near = []
    for pair in range(pairs):
        logits = dot(queries[rows_of(pair), :], table[...])
        top, probs = weigh(logits, bias[:, 0:points], inverse)
        near.append((join_heads(top), *mix(probs, values[:, lanes_of(pair)])))

    loaded(pq_v, pk_v, pv_v, po_v)
    for copy in weight_copies:
        copy.wait_recv()
    processor = (pq_v, pk_v, pv_v)
    sums = []
    for index, weight in enumerate(processor):
        w_joint[index] = dot(w_other[...], weight[...]).astype(BF16)
        sums.append(dot(jnp.ones((8, width), BF16), weight[...])[0:1])

    loaded(wo_v)
    pl.when(late > 0)(lambda: pl.semaphore_wait(wrap_sem, 2 * late))
    for slot in behind:
        pl.when(region + offset_of(slot) < 0)(functools.partial(send_list, slot))
    for slot in range(NEIGH):
        for copy in list_copies(slot):
            copy.wait_recv()
    far = received[0] + received[1]
    far_twice = jnp.concatenate([far, far], axis=1)
    squares = dot(far_twice, gram_down) * far.astype(F32)
    inverse = inverse_of(squares.T, 0)
    middle = pairs * nodes
    far_logits = jnp.concatenate(
        [dot(queries[0:middle, :], far_twice, NT), dot(queries[middle:, :], far_twice, NT)], axis=0
    )
    far_weights = [
        weigh(far_logits[rows_of(pair)], bias[:, points : points + remote], inverse)
        for pair in range(pairs)
    ]
    far_values = values_of(far, inverse_of(squares, 1))
    for pair in range(pairs):
        lanes = lanes_of(pair)
        top, probs = far_weights[pair]
        mixed, total = mix(probs, far_values[:, lanes])
        near_top, near_mixed, near_total = near[pair]
        top = join_heads(top)
        best = jnp.maximum(top, near_top)
        gain, near_gain = jnp.exp2(top - best), jnp.exp2(near_top - best)
        both = gain * mixed + near_gain * near_mixed
        context[:, lanes] = (both / (gain * total + near_gain * near_total)).astype(BF16)

    sum_copy = pltpu.make_async_remote_copy(
        src_ref=context, dst_ref=context_in, send_sem=sum_send.at[0], recv_sem=sum_recv.at[0],
        device_id=twin, device_id_type=MESH,
    )
    sum_copy.start()
    start = mesh_v[...].astype(F32) + dot(context[...], wo_v[...])
    shift = jnp.mean(start, axis=-1, keepdims=True)
    start = start - shift
    hidden[...] = start
    start = start.astype(BF16)
    for index, weight in enumerate(processor):
        ahead_sum[index] = dot(start, weight[...])
    sum_copy.wait_recv()

    theirs_in = context_in[...]
    centred = hidden[...] + dot(theirs_in, w_other[...])
    mean = jnp.mean(centred, axis=-1, keepdims=True)
    hidden[...] = centred + shift
    spread = jnp.mean(centred * centred, axis=-1, keepdims=True) - mean * mean
    rise = lax.rsqrt(jnp.maximum(spread, 0.0) + 1e-05)

    raw = [ahead_sum[index] + dot(theirs_in, w_joint[index]) for index in range(3)]

    def projected(index):
        return ((raw[index] - mean * sums[index]) * rise).astype(BF16)

    proc_q, proc_k = projected(0), projected(1)
    probs = []
    for pair in range(pairs):
        lanes = lanes_of(pair)
        logits = dot(two_heads(proc_q[:, lanes]), proc_k[:, lanes], NT) * exponent
        probs.append(jnp.exp2(logits - jnp.max(logits, axis=-1, keepdims=True)).astype(BF16))
    proc_v = projected(2)
    for pair in range(pairs):
        lanes = lanes_of(pair)
        mixed, total = mix(probs[pair], proc_v[:, lanes])
        context_late[:, lanes] = (mixed / total).astype(BF16)

    theirs = pl.ds(pl.multiple_of((1 - core) * own_rows, own_rows), own_rows)
    mine = pl.ds(pl.multiple_of(core * own_rows, own_rows), own_rows)
    last_copy = pltpu.make_async_remote_copy(
        src_ref=context_late.at[theirs], dst_ref=last_in, send_sem=last_sem.at[0],
        recv_sem=last_sem.at[1], device_id=twin, device_id_type=MESH,
    )
    last_copy.start()
    tail[...] = hidden[mine, :] + dot(context_late[mine, :], po_v[...])
    last_copy.wait_recv()
    out[...] = (tail[...] + dot(last_in[...], p_other[...])).astype(BF16)
    for copy in [half_copy, *weight_copies, sum_copy, last_copy]:
        copy.wait_send()
    for slot in range(NEIGH):
        for copy in list_copies(slot):
            copy.wait_send()


def local(*args):
    args = args[:12] + (args[12].T, args[13].T)
    fields, mesh_state = args[0], args[1]
    send_rows = args[11]
    ch, half = fields.shape
    nodes, width = mesh_state.shape
    cols = args[3].shape[1]
    pairs = cols // LANES
    remote = send_rows.shape[1] * send_rows.shape[2]
    columns = 2 * half + remote
    copies = [pltpu.VMEM(x.shape, x.dtype) for x in args]
    buffers = [
        pltpu.VMEM((ch, half), BF16),
        pltpu.VMEM((remote, LANES), BF16),
        pltpu.VMEM((2, remote, LANES), BF16),
        pltpu.VMEM((2 * LANES, 2 * half), BF16),
        pltpu.VMEM((2 * half, LANES), BF16),
        pltpu.VMEM((2 * half, cols), BF16),
        pltpu.VMEM((nodes, columns), F32),
        pltpu.VMEM((pairs * 2 * nodes, 2 * LANES), BF16),
        pltpu.VMEM((nodes, width), F32),
        pltpu.VMEM((nodes, cols), BF16),
        pltpu.VMEM((nodes // 2, width), F32),
        pltpu.VMEM((nodes // 2, cols), BF16),
        pltpu.VMEM((cols, width), BF16),
        pltpu.VMEM((cols, width), BF16),
        pltpu.VMEM((3, cols, cols), BF16),
        pltpu.VMEM((nodes, cols), BF16),
        pltpu.VMEM((3, nodes, cols), F32),
        pltpu.VMEM((nodes, cols), BF16),
    ]
    semaphores = [
        pltpu.SemaphoreType.DMA((len(args),)),
        pltpu.SemaphoreType.DMA((2,)),
        pltpu.SemaphoreType.DMA((2 * NEIGH,)),
        pltpu.SemaphoreType.DMA((2 * NEIGH,)),
        pltpu.SemaphoreType.DMA((2,)),
        pltpu.SemaphoreType.DMA((2,)),
        pltpu.SemaphoreType.DMA((1,)),
        pltpu.SemaphoreType.DMA((1,)),
        pltpu.SemaphoreType.DMA((2,)),
    ] + [pltpu.SemaphoreType.REGULAR]
    return pl.pallas_call(
        kernel,
        out_shape=pltpu.VMEM((nodes // 2, width), BF16),
        in_specs=[pl.BlockSpec(memory_space=pltpu.HBM)] * len(args),
        out_specs=pl.BlockSpec(memory_space=pltpu.VMEM),
        scratch_shapes=copies + buffers + semaphores,
        compiler_params=pltpu.CompilerParams(
            collective_id=0, has_side_effects=True, vmem_limit_bytes=56 * 1024 * 1024
        ),
        cost_estimate=pl.CostEstimate(
            flops=3_000_000_000, bytes_accessed=9_500_000, transcendentals=800_000
        ),
        name="encode_and_process",
    )(*args)


def solution(mesh):
    return jax.shard_map(
        local,
        mesh=mesh,
        in_specs=(
            P(None, ("nodes", "heads")),
            P("nodes", None),
            P(),
            P(None, "heads"),
            P(None, "heads"),
            P(None, "heads"),
            P("heads", None),
            P(None, "heads"),
            P(None, "heads"),
            P(None, "heads"),
            P("heads", None),
            P("nodes", None, None),
            P("nodes", None),
            P("nodes", None),
        ),
        out_specs=P(("nodes", "heads"), None),
        check_vma=False,
    )
```

```python
import functools
import math

import jax
import jax.numpy as jnp
from jax import lax
from jax.experimental import pallas as pl
from jax.experimental.pallas import tpu as pltpu
from jax.sharding import PartitionSpec as P

HEADS = 16
HS = 64
NEIGH = 4
F32 = jnp.float32
BF16 = jnp.bfloat16
MESH = pl.DeviceIdType.MESH
LANES = 128
LOG2E = math.log2(math.e)
NN = (((1,), (0,)), ((), ()))
NT = (((1,), (1,)), ((), ()))


def offset_of(slot):
    return (slot // 2 + 1) * (1 if slot % 2 == 0 else -1)


def dot(a, b, dims=NN):
    return lax.dot_general(a, b, dims, preferred_element_type=F32)


def split(x):
    high = x.astype(BF16)
    return high, (x - high.astype(F32)).astype(BF16)


def normalize(x):
    centred = x - jnp.mean(x, axis=-1, keepdims=True)
    spread = jnp.mean(centred * centred, axis=-1, keepdims=True)
    return centred * lax.rsqrt(spread + 1e-05)


def iota(shape, axis):
    return lax.broadcasted_iota(jnp.int32, shape, axis)


def kernel(
    fields, mesh_state, w_embed, w_q, w_k, w_v, w_o, p_q, p_k, p_v, p_o, send_rows, senders, mask,
    out,
    own_v, mesh_v, embed_v, wq_v, wk_v, wv_v, wo_v, pq_v, pk_v, pv_v, po_v, rows_v, send_v, mask_v,
    other_v, listed, received, table, last, values, bias, queries, hidden,     context, tail, last_in, w_other, p_other, w_joint, context_in, ahead_sum,
    context_late,
    load_sem, half_sem, list_send, list_recv, weight_send, weight_recv, sum_send, sum_recv, last_sem,
    wrap_sem,
):
    n = lax.axis_size("nodes")
    region, core = lax.axis_index("nodes"), lax.axis_index("heads")
    twin = {"nodes": region, "heads": 1 - core}
    ch, half = fields.shape
    nodes, width = mesh_state.shape
    fan = senders.shape[0]
    cols = w_q.shape[1]
    pairs = cols // LANES
    cap = send_rows.shape[2]
    points = 2 * half
    remote = NEIGH * cap
    own_rows = nodes // 2
    exponent = LOG2E / math.sqrt(HS)

    def neighbour(slot, other):
        place = lax.rem(region + (offset_of(slot) + n), n)
        return {"nodes": place, "heads": 1 - core if other else core}

    loads = {}
    pieces = [
        (fields, own_v), (send_rows, rows_v), (w_embed, embed_v), (senders, send_v), (mask, mask_v),
        (mesh_state, mesh_v), (w_q, wq_v), (w_k, wk_v), (w_v, wv_v), (w_o, wo_v),
        (p_q, pq_v), (p_k, pk_v), (p_v, pv_v), (p_o, po_v),
    ]
    for index, (source, target) in enumerate(pieces):
        loads[id(target)] = pltpu.make_async_copy(source, target, load_sem.at[index])

    def loaded(*targets):
        for target in targets:
            loads.pop(id(target)).wait()

    for _, target in pieces[:3]:
        loads[id(target)].start()
    barrier = pltpu.get_barrier_semaphore()

    def greet(slot, semaphore):
        for other in range(2):
            pl.semaphore_signal(
                semaphore, inc=1, device_id=neighbour(slot, other), device_id_type=MESH
            )

    pl.semaphore_signal(barrier, inc=1, device_id=twin, device_id_type=MESH)
    for slot in range(NEIGH):
        if offset_of(slot) < 0:
            greet(slot, barrier)
        else:
            pl.when(region + offset_of(slot) < n)(functools.partial(greet, slot, barrier))
    late = sum((region + offset_of(slot) < 0).astype(jnp.int32) for slot in range(NEIGH))
    for _, target in pieces[3:]:
        loads[id(target)].start()

    loaded(own_v, rows_v)
    widen = (iota((LANES, ch), 0) == iota((LANES, ch), 1)).astype(BF16)
    own = dot(widen, own_v[...]).astype(BF16)
    rows = rows_v[0]
    wanted = jnp.concatenate([rows[j : j + 1, :] for j in range(NEIGH)], axis=1) - core * half
    pick = (iota((half, remote), 0) == wanted).astype(BF16)
    listed[...] = dot(own, pick).T.astype(BF16)

    pl.semaphore_wait(barrier, 1 + 2 * NEIGH - 2 * late)
    def list_copies(slot):
        part = pl.ds(slot * cap, cap)
        return [
            pltpu.make_async_remote_copy(
                src_ref=listed.at[part], dst_ref=received.at[other, part],
                send_sem=list_send.at[2 * slot + other], recv_sem=list_recv.at[2 * slot + other],
                device_id=neighbour(slot, other), device_id_type=MESH,
            )
            for other in range(2)
        ]

    def send_list(slot):
        for copy in list_copies(slot):
            copy.start()

    ahead = [slot for slot in range(NEIGH) if offset_of(slot) > 0]
    behind = [slot for slot in range(NEIGH) if offset_of(slot) < 0]
    for slot in ahead:
        send_list(slot)
    for slot in ahead:
        pl.when(region + offset_of(slot) >= n)(functools.partial(greet, slot, wrap_sem))
    for slot in behind:
        pl.when(region + offset_of(slot) >= 0)(functools.partial(send_list, slot))
    half_copy = pltpu.make_async_remote_copy(
        src_ref=fields, dst_ref=other_v, send_sem=half_sem.at[0], recv_sem=half_sem.at[1],
        device_id=twin, device_id_type=MESH,
    )
    half_copy.start()
    weight_copies = [
        pltpu.make_async_remote_copy(
            src_ref=source, dst_ref=target, send_sem=weight_send.at[index],
            recv_sem=weight_recv.at[index], device_id=twin, device_id_type=MESH,
        )
        for index, (source, target) in enumerate([(w_o, w_other), (p_o, p_other)])
    ]
    for copy in weight_copies:
        copy.start()

    loaded(embed_v)
    embed = dot(widen, embed_v[...])
    embed = jnp.where(iota((LANES, 1), 0) == ch, 1.0, embed).astype(BF16)
    gram = dot(embed, embed, NT) * (1.0 / width)
    mean = gram[:, ch : ch + 1]
    gram = split(gram - mean * gram[ch : ch + 1, :])
    gram_down = jnp.concatenate(gram, axis=0)
    gram = jnp.concatenate(gram, axis=1)

    def through(weight):
        both = dot(embed, weight[...])
        return split(both - mean * both[ch : ch + 1, :])

    def inverse_of(squares, axis):
        squares = jnp.maximum(jnp.sum(squares, axis=axis, keepdims=True), 0.0)
        return lax.rsqrt(squares + 1e-05)

    def place_half(block, first):
        twice = jnp.concatenate([block, block], axis=0)
        table[:, first : first + half] = twice
        block = block.astype(F32)
        squares = dot(gram, twice) * block
        last[first : first + half, :] = block.T.astype(BF16)
        return inverse_of(squares, 0), inverse_of(squares.T, 1)

    inverse, scale = place_half(own, 0)

    loaded(send_v, mask_v)
    spot = send_v[...]
    tiles = (points + remote) // LANES
    word = jnp.zeros_like(spot)
    for tile in range(tiles):
        word = jnp.where(spot >= tile * LANES, 1 << (6 * tile), word)
    word = jnp.where(mask_v[...] > 0, word, 0)
    spot = spot & (LANES - 1)
    down = iota((LANES, nodes), 0)
    counts = jnp.zeros((LANES, nodes), jnp.int32)
    for slot in range(fan):
        counts += jnp.where(spot[slot : slot + 1, :] == down, word[slot : slot + 1, :], 0)
    counts = counts.T
    for tile in range(tiles):
        total = ((counts >> (6 * tile)) & 63).astype(F32)
        total = jnp.where(total > 0, jnp.log2(jnp.maximum(total, 1.0)), -1e30)
        first = tile * LANES
        if first < points:
            first = lax.rem(first + core * half, points)
        bias[:, pl.ds(pl.multiple_of(first, LANES), LANES)] = total

    loaded(mesh_v, wq_v)
    normed = normalize(mesh_v[...].astype(F32)).astype(BF16)
    enc_queries = dot(normed, wq_v[...]).astype(BF16)

    loaded(wk_v)
    k_high, k_low = through(wk_v)
    low_lanes = iota((nodes, LANES), 1) < HS

    def lanes_of(pair):
        return slice(pair * LANES, (pair + 1) * LANES)

    def rows_of(pair):
        return slice(2 * pair * nodes, 2 * (pair + 1) * nodes)

    def two_heads(rows):
        zeros = jnp.zeros_like(rows)
        even, odd = jnp.where(low_lanes, rows, zeros), jnp.where(low_lanes, zeros, rows)
        return jnp.concatenate([even, odd], axis=0)

    for pair in range(pairs):
        lanes = lanes_of(pair)
        two = two_heads(enc_queries[:, lanes])
        keys = jnp.concatenate([k_high[:, lanes], k_low[:, lanes]], axis=1)
        high, low = split(dot(jnp.concatenate([two, two], axis=1), keys, NT))
        queries[rows_of(pair), 0:LANES] = high
        queries[rows_of(pair), LANES : 2 * LANES] = low

    loaded(wv_v)
    v_both = jnp.concatenate(through(wv_v), axis=0)

    def values_of(rows, scale):
        return (dot(jnp.concatenate([rows, rows], axis=1), v_both) * scale).astype(BF16)

    def weigh(logits, edges, inverse):
        logits = logits * (inverse * exponent) + jnp.concatenate([edges, edges], axis=0)
        top = jnp.max(logits, axis=-1, keepdims=True)
        return top, jnp.exp2(logits - top).astype(BF16)

    def join_heads(rows):
        return jnp.where(low_lanes, rows[:nodes], rows[nodes:])

    def mix(probs, values):
        mixed = dot(probs, jnp.concatenate([values, jnp.ones_like(values)], axis=1))
        return join_heads(mixed[:, :LANES]), join_heads(mixed[:, LANES:])

    half_copy.wait_recv()
    other_inverse, other_scale = place_half(dot(widen, other_v[...]).astype(BF16), half)
    inverse = jnp.concatenate([inverse, other_inverse], axis=1)
    values[0:half, :] = values_of(last[0:half, :], scale)
    values[half:points, :] = values_of(last[half:points, :], other_scale)
    near = []
    for pair in range(pairs):
        logits = dot(queries[rows_of(pair), :], table[...])
        top, probs = weigh(logits, bias[:, 0:points], inverse)
        near.append((join_heads(top), *mix(probs, values[:, lanes_of(pair)])))

    shift = jnp.mean(mesh_v[...].astype(F32), axis=-1, keepdims=True)

    loaded(pq_v, pk_v, pv_v, po_v)
    for copy in weight_copies:
        copy.wait_recv()
    processor = (pq_v, pk_v, pv_v)
    sums = []
    for index, weight in enumerate(processor):
        w_joint[index] = dot(w_other[...], weight[...]).astype(BF16)
        sums.append(dot(jnp.ones((8, width), BF16), weight[...])[0:1])

    loaded(wo_v)
    pl.when(late > 0)(lambda: pl.semaphore_wait(wrap_sem, 2 * late))
    for slot in behind:
        pl.when(region + offset_of(slot) < 0)(functools.partial(send_list, slot))
    for slot in range(NEIGH):
        for copy in list_copies(slot):
            copy.wait_recv()
    far = received[0] + received[1]
    far_twice = jnp.concatenate([far, far], axis=1)
    squares = dot(far_twice, gram_down) * far.astype(F32)
    inverse = inverse_of(squares.T, 0)
    middle = pairs * nodes
    far_logits = jnp.concatenate(
        [dot(queries[0:middle, :], far_twice, NT), dot(queries[middle:, :], far_twice, NT)], axis=0
    )
    far_weights = [
        weigh(far_logits[rows_of(pair)], bias[:, points : points + remote], inverse)
        for pair in range(pairs)
    ]
    far_values = values_of(far, inverse_of(squares, 1))
    for pair in range(pairs):
        lanes = lanes_of(pair)
        top, probs = far_weights[pair]
        mixed, total = mix(probs, far_values[:, lanes])
        near_top, near_mixed, near_total = near[pair]
        top = join_heads(top)
        best = jnp.maximum(top, near_top)
        gain, near_gain = jnp.exp2(top - best), jnp.exp2(near_top - best)
        both = gain * mixed + near_gain * near_mixed
        context[:, lanes] = (both / (gain * total + near_gain * near_total)).astype(BF16)

    sum_copy = pltpu.make_async_remote_copy(
        src_ref=context, dst_ref=context_in, send_sem=sum_send.at[0], recv_sem=sum_recv.at[0],
        device_id=twin, device_id_type=MESH,
    )
    sum_copy.start()
    start = mesh_v[...].astype(F32) - shift + dot(context[...], wo_v[...])
    hidden[...] = start
    start = start.astype(BF16)
    for index, weight in enumerate(processor):
        ahead_sum[index] = dot(start, weight[...])
    sum_copy.wait_recv()

    theirs_in = context_in[...]
    centred = hidden[...] + dot(theirs_in, w_other[...])
    mean = jnp.mean(centred, axis=-1, keepdims=True)
    hidden[...] = centred + shift
    spread = jnp.mean(centred * centred, axis=-1, keepdims=True) - mean * mean
    rise = lax.rsqrt(jnp.maximum(spread, 0.0) + 1e-05)

    raw = [ahead_sum[index] + dot(theirs_in, w_joint[index]) for index in range(3)]

    def projected(index):
        return ((raw[index] - mean * sums[index]) * rise).astype(BF16)

    proc_q, proc_k = projected(0), projected(1)
    probs = []
    for pair in range(pairs):
        lanes = lanes_of(pair)
        logits = dot(two_heads(proc_q[:, lanes]), proc_k[:, lanes], NT) * exponent
        probs.append(jnp.exp2(logits - jnp.max(logits, axis=-1, keepdims=True)).astype(BF16))
    proc_v = projected(2)
    for pair in range(pairs):
        lanes = lanes_of(pair)
        mixed, total = mix(probs[pair], proc_v[:, lanes])
        context_late[:, lanes] = (mixed / total).astype(BF16)

    theirs = pl.ds(pl.multiple_of((1 - core) * own_rows, own_rows), own_rows)
    mine = pl.ds(pl.multiple_of(core * own_rows, own_rows), own_rows)
    last_copy = pltpu.make_async_remote_copy(
        src_ref=context_late.at[theirs], dst_ref=last_in, send_sem=last_sem.at[0],
        recv_sem=last_sem.at[1], device_id=twin, device_id_type=MESH,
    )
    last_copy.start()
    tail[...] = hidden[mine, :] + dot(context_late[mine, :], po_v[...])
    last_copy.wait_recv()
    out[...] = (tail[...] + dot(last_in[...], p_other[...])).astype(BF16)
    for copy in [half_copy, *weight_copies, sum_copy, last_copy]:
        copy.wait_send()
    for slot in range(NEIGH):
        for copy in list_copies(slot):
            copy.wait_send()


def local(*args):
    args = args[:12] + (args[12].T, args[13].T)
    fields, mesh_state = args[0], args[1]
    send_rows = args[11]
    ch, half = fields.shape
    nodes, width = mesh_state.shape
    cols = args[3].shape[1]
    pairs = cols // LANES
    remote = send_rows.shape[1] * send_rows.shape[2]
    columns = 2 * half + remote
    copies = [pltpu.VMEM(x.shape, x.dtype) for x in args]
    buffers = [
        pltpu.VMEM((ch, half), BF16),
        pltpu.VMEM((remote, LANES), BF16),
        pltpu.VMEM((2, remote, LANES), BF16),
        pltpu.VMEM((2 * LANES, 2 * half), BF16),
        pltpu.VMEM((2 * half, LANES), BF16),
        pltpu.VMEM((2 * half, cols), BF16),
        pltpu.VMEM((nodes, columns), F32),
        pltpu.VMEM((pairs * 2 * nodes, 2 * LANES), BF16),
        pltpu.VMEM((nodes, width), F32),
        pltpu.VMEM((nodes, cols), BF16),
        pltpu.VMEM((nodes // 2, width), F32),
        pltpu.VMEM((nodes // 2, cols), BF16),
        pltpu.VMEM((cols, width), BF16),
        pltpu.VMEM((cols, width), BF16),
        pltpu.VMEM((3, cols, cols), BF16),
        pltpu.VMEM((nodes, cols), BF16),
        pltpu.VMEM((3, nodes, cols), F32),
        pltpu.VMEM((nodes, cols), BF16),
    ]
    semaphores = [
        pltpu.SemaphoreType.DMA((len(args),)),
        pltpu.SemaphoreType.DMA((2,)),
        pltpu.SemaphoreType.DMA((2 * NEIGH,)),
        pltpu.SemaphoreType.DMA((2 * NEIGH,)),
        pltpu.SemaphoreType.DMA((2,)),
        pltpu.SemaphoreType.DMA((2,)),
        pltpu.SemaphoreType.DMA((1,)),
        pltpu.SemaphoreType.DMA((1,)),
        pltpu.SemaphoreType.DMA((2,)),
    ] + [pltpu.SemaphoreType.REGULAR]
    return pl.pallas_call(
        kernel,
        out_shape=pltpu.VMEM((nodes // 2, width), BF16),
        in_specs=[pl.BlockSpec(memory_space=pltpu.HBM)] * len(args),
        out_specs=pl.BlockSpec(memory_space=pltpu.VMEM),
        scratch_shapes=copies + buffers + semaphores,
        compiler_params=pltpu.CompilerParams(
            collective_id=0, has_side_effects=True, vmem_limit_bytes=56 * 1024 * 1024
        ),
        cost_estimate=pl.CostEstimate(
            flops=3_000_000_000, bytes_accessed=9_500_000, transcendentals=800_000
        ),
        name="encode_and_process",
    )(*args)


def solution(mesh):
    return jax.shard_map(
        local,
        mesh=mesh,
        in_specs=(
            P(None, ("nodes", "heads")),
            P("nodes", None),
            P(),
            P(None, "heads"),
            P(None, "heads"),
            P(None, "heads"),
            P("heads", None),
            P(None, "heads"),
            P(None, "heads"),
            P(None, "heads"),
            P("heads", None),
            P("nodes", None, None),
            P("nodes", None),
            P("nodes", None),
        ),
        out_specs=P(("nodes", "heads"), None),
        check_vma=False,
    )
```

```python
import functools
import math

import jax
import jax.numpy as jnp
from jax import lax
from jax.experimental import pallas as pl
from jax.experimental.pallas import tpu as pltpu
from jax.sharding import PartitionSpec as P

HEADS = 16
HS = 64
NEIGH = 4
F32 = jnp.float32
BF16 = jnp.bfloat16
MESH = pl.DeviceIdType.MESH
LANES = 128
LOG2E = math.log2(math.e)
NN = (((1,), (0,)), ((), ()))
NT = (((1,), (1,)), ((), ()))


def offset_of(slot):
    return (slot // 2 + 1) * (1 if slot % 2 == 0 else -1)


def dot(a, b, dims=NN):
    return lax.dot_general(a, b, dims, preferred_element_type=F32)


def split(x):
    high = x.astype(BF16)
    return high, (x - high.astype(F32)).astype(BF16)


def normalize(x):
    centred = x - jnp.mean(x, axis=-1, keepdims=True)
    spread = jnp.mean(centred * centred, axis=-1, keepdims=True)
    return centred * lax.rsqrt(spread + 1e-05)


def iota(shape, axis):
    return lax.broadcasted_iota(jnp.int32, shape, axis)


def kernel(
    fields, mesh_state, w_embed, w_q, w_k, w_v, w_o, p_q, p_k, p_v, p_o, send_rows, senders, mask,
    out,
    own_v, mesh_v, embed_v, wq_v, wk_v, wv_v, wo_v, pq_v, pk_v, pv_v, po_v, rows_v, send_v, mask_v,
    other_v, listed, received, table, last, values, bias, queries, hidden,     context, tail, last_in, w_other, p_other, w_joint, context_in, ahead_sum,
    context_late,
    load_sem, half_sem, list_send, list_recv, weight_send, weight_recv, sum_send, sum_recv, last_sem,
    wrap_sem, late_sem,
):
    n = lax.axis_size("nodes")
    region, core = lax.axis_index("nodes"), lax.axis_index("heads")
    twin = {"nodes": region, "heads": 1 - core}
    ch, half = fields.shape
    nodes, width = mesh_state.shape
    fan = senders.shape[0]
    cols = w_q.shape[1]
    pairs = cols // LANES
    cap = send_rows.shape[2]
    points = 2 * half
    remote = NEIGH * cap
    own_rows = nodes // 2
    exponent = LOG2E / math.sqrt(HS)

    def neighbour(slot, other):
        place = lax.rem(region + (offset_of(slot) + n), n)
        return {"nodes": place, "heads": 1 - core if other else core}

    loads = {}
    pieces = [
        (fields, own_v), (send_rows, rows_v), (w_embed, embed_v), (senders, send_v), (mask, mask_v),
        (mesh_state, mesh_v), (w_q, wq_v), (w_k, wk_v), (w_v, wv_v), (w_o, wo_v),
        (p_q, pq_v), (p_k, pk_v), (p_v, pv_v), (p_o, po_v),
    ]
    for index, (source, target) in enumerate(pieces):
        loads[id(target)] = pltpu.make_async_copy(source, target, load_sem.at[index])

    def loaded(*targets):
        for target in targets:
            loads.pop(id(target)).wait()

    for _, target in pieces[:3]:
        loads[id(target)].start()
    barrier = pltpu.get_barrier_semaphore()
    edge = n - 2
    ahead = [slot for slot in range(NEIGH) if offset_of(slot) > 0]
    behind = [slot for slot in range(NEIGH) if offset_of(slot) < 0]
    late = sum((region + offset_of(slot) < 0).astype(jnp.int32) for slot in behind)
    wraps = sum((region + offset_of(slot) >= n).astype(jnp.int32) for slot in ahead)
    feeds = sum((region - offset_of(slot) < edge).astype(jnp.int32) for slot in ahead)
    in_last = (region >= edge).astype(jnp.int32)

    def greet(slot, semaphore):
        for other in range(2):
            pl.semaphore_signal(
                semaphore, inc=1, device_id=neighbour(slot, other), device_id_type=MESH
            )

    @pl.when(region < edge)
    def _():
        pl.semaphore_signal(barrier, inc=1, device_id=twin, device_id_type=MESH)

    for slot in range(NEIGH):
        place = region + offset_of(slot)
        if slot in ahead:
            pl.when(place < edge)(functools.partial(greet, slot, barrier))
        else:
            pl.when((region < edge) | (place < edge))(functools.partial(greet, slot, barrier))
    for _, target in pieces[3:]:
        loads[id(target)].start()

    loaded(own_v, rows_v)
    widen = (iota((LANES, ch), 0) == iota((LANES, ch), 1)).astype(BF16)
    own = dot(widen, own_v[...]).astype(BF16)
    rows = rows_v[0]
    wanted = jnp.concatenate([rows[j : j + 1, :] for j in range(NEIGH)], axis=1) - core * half
    pick = (iota((half, remote), 0) == wanted).astype(BF16)
    listed[...] = dot(own, pick).T.astype(BF16)

    pl.semaphore_wait(barrier, (1 - in_last) * (1 + 2 * NEIGH - 2 * late) + in_last * 2 * wraps)

    def list_copies(slot):
        part = pl.ds(slot * cap, cap)
        return [
            pltpu.make_async_remote_copy(
                src_ref=listed.at[part], dst_ref=received.at[other, part],
                send_sem=list_send.at[2 * slot + other], recv_sem=list_recv.at[2 * slot + other],
                device_id=neighbour(slot, other), device_id_type=MESH,
            )
            for other in range(2)
        ]

    def send_list(slot):
        for copy in list_copies(slot):
            copy.start()

    for slot in ahead:
        place = region + offset_of(slot)
        pl.when((region < edge) | (place >= n))(functools.partial(send_list, slot))
    for slot in ahead:
        place = region + offset_of(slot)
        pl.when(place >= n)(functools.partial(greet, slot, wrap_sem))
        pl.when((region < edge) & (place >= edge))(functools.partial(greet, slot, late_sem))
    pl.when(region >= edge)(lambda: pl.semaphore_wait(late_sem, 2 * feeds))
    for slot in ahead:
        place = region + offset_of(slot)
        pl.when((region >= edge) & (place < n))(functools.partial(send_list, slot))
    for slot in behind:
        pl.when(region + offset_of(slot) >= 0)(functools.partial(send_list, slot))
    half_copy = pltpu.make_async_remote_copy(
        src_ref=fields, dst_ref=other_v, send_sem=half_sem.at[0], recv_sem=half_sem.at[1],
        device_id=twin, device_id_type=MESH,
    )
    half_copy.start()
    weight_copies = [
        pltpu.make_async_remote_copy(
            src_ref=source, dst_ref=target, send_sem=weight_send.at[index],
            recv_sem=weight_recv.at[index], device_id=twin, device_id_type=MESH,
        )
        for index, (source, target) in enumerate([(w_o, w_other), (p_o, p_other)])
    ]
    for copy in weight_copies:
        copy.start()

    loaded(embed_v)
    embed = dot(widen, embed_v[...])
    embed = jnp.where(iota((LANES, 1), 0) == ch, 1.0, embed).astype(BF16)
    gram = dot(embed, embed, NT) * (1.0 / width)
    mean = gram[:, ch : ch + 1]
    gram = split(gram - mean * gram[ch : ch + 1, :])
    gram_down = jnp.concatenate(gram, axis=0)
    gram = jnp.concatenate(gram, axis=1)

    def through(weight):
        both = dot(embed, weight[...])
        return split(both - mean * both[ch : ch + 1, :])

    def inverse_of(squares, axis):
        squares = jnp.maximum(jnp.sum(squares, axis=axis, keepdims=True), 0.0)
        return lax.rsqrt(squares + 1e-05)

    def place_half(block, first):
        twice = jnp.concatenate([block, block], axis=0)
        table[:, first : first + half] = twice
        block = block.astype(F32)
        squares = dot(gram, twice) * block
        last[first : first + half, :] = block.T.astype(BF16)
        return inverse_of(squares, 0), inverse_of(squares.T, 1)

    inverse, scale = place_half(own, 0)

    loaded(send_v, mask_v)
    spot = send_v[...]
    tiles = (points + remote) // LANES
    word = jnp.zeros_like(spot)
    for tile in range(tiles):
        word = jnp.where(spot >= tile * LANES, 1 << (6 * tile), word)
    word = jnp.where(mask_v[...] > 0, word, 0)
    spot = spot & (LANES - 1)
    down = iota((LANES, nodes), 0)
    counts = jnp.zeros((LANES, nodes), jnp.int32)
    for slot in range(fan):
        counts += jnp.where(spot[slot : slot + 1, :] == down, word[slot : slot + 1, :], 0)
    counts = counts.T
    for tile in range(tiles):
        total = ((counts >> (6 * tile)) & 63).astype(F32)
        total = jnp.where(total > 0, jnp.log2(jnp.maximum(total, 1.0)), -1e30)
        first = tile * LANES
        if first < points:
            first = lax.rem(first + core * half, points)
        bias[:, pl.ds(pl.multiple_of(first, LANES), LANES)] = total

    loaded(mesh_v, wq_v)
    normed = normalize(mesh_v[...].astype(F32)).astype(BF16)
    enc_queries = dot(normed, wq_v[...]).astype(BF16)

    loaded(wk_v)
    k_high, k_low = through(wk_v)
    low_lanes = iota((nodes, LANES), 1) < HS

    def lanes_of(pair):
        return slice(pair * LANES, (pair + 1) * LANES)

    def rows_of(pair):
        return slice(2 * pair * nodes, 2 * (pair + 1) * nodes)

    def two_heads(rows):
        zeros = jnp.zeros_like(rows)
        even, odd = jnp.where(low_lanes, rows, zeros), jnp.where(low_lanes, zeros, rows)
        return jnp.concatenate([even, odd], axis=0)

    for pair in range(pairs):
        lanes = lanes_of(pair)
        two = two_heads(enc_queries[:, lanes])
        keys = jnp.concatenate([k_high[:, lanes], k_low[:, lanes]], axis=1)
        high, low = split(dot(jnp.concatenate([two, two], axis=1), keys, NT))
        queries[rows_of(pair), 0:LANES] = high
        queries[rows_of(pair), LANES : 2 * LANES] = low

    loaded(wv_v)
    v_both = jnp.concatenate(through(wv_v), axis=0)

    def values_of(rows, scale):
        return (dot(jnp.concatenate([rows, rows], axis=1), v_both) * scale).astype(BF16)

    def weigh(logits, edges, inverse):
        logits = logits * (inverse * exponent) + jnp.concatenate([edges, edges], axis=0)
        top = jnp.max(logits, axis=-1, keepdims=True)
        return top, jnp.exp2(logits - top).astype(BF16)

    def join_heads(rows):
        return jnp.where(low_lanes, rows[:nodes], rows[nodes:])

    def mix(probs, values):
        mixed = dot(probs, jnp.concatenate([values, jnp.ones_like(values)], axis=1))
        return join_heads(mixed[:, :LANES]), join_heads(mixed[:, LANES:])

    half_copy.wait_recv()
    other_inverse, other_scale = place_half(dot(widen, other_v[...]).astype(BF16), half)
    inverse = jnp.concatenate([inverse, other_inverse], axis=1)
    values[0:half, :] = values_of(last[0:half, :], scale)
    values[half:points, :] = values_of(last[half:points, :], other_scale)
    near = []
    for pair in range(pairs):
        logits = dot(queries[rows_of(pair), :], table[...])
        top, probs = weigh(logits, bias[:, 0:points], inverse)
        near.append((join_heads(top), *mix(probs, values[:, lanes_of(pair)])))

    shift = jnp.mean(mesh_v[...].astype(F32), axis=-1, keepdims=True)

    loaded(pq_v, pk_v, pv_v, po_v)
    for copy in weight_copies:
        copy.wait_recv()
    processor = (pq_v, pk_v, pv_v)
    sums = []
    for index, weight in enumerate(processor):
        w_joint[index] = dot(w_other[...], weight[...]).astype(BF16)
        sums.append(dot(jnp.ones((8, width), BF16), weight[...])[0:1])

    loaded(wo_v)
    pl.when(late > 0)(lambda: pl.semaphore_wait(wrap_sem, 2 * late))
    for slot in behind:
        pl.when(region + offset_of(slot) < 0)(functools.partial(send_list, slot))
    for slot in range(NEIGH):
        for copy in list_copies(slot):
            copy.wait_recv()
    far = received[0] + received[1]
    far_twice = jnp.concatenate([far, far], axis=1)
    squares = dot(far_twice, gram_down) * far.astype(F32)
    inverse = inverse_of(squares.T, 0)
    middle = pairs * nodes
    far_logits = jnp.concatenate(
        [dot(queries[0:middle, :], far_twice, NT), dot(queries[middle:, :], far_twice, NT)], axis=0
    )
    far_weights = [
        weigh(far_logits[rows_of(pair)], bias[:, points : points + remote], inverse)
        for pair in range(pairs)
    ]
    far_values = values_of(far, inverse_of(squares, 1))
    for pair in range(pairs):
        lanes = lanes_of(pair)
        top, probs = far_weights[pair]
        mixed, total = mix(probs, far_values[:, lanes])
        near_top, near_mixed, near_total = near[pair]
        top = join_heads(top)
        best = jnp.maximum(top, near_top)
        gain, near_gain = jnp.exp2(top - best), jnp.exp2(near_top - best)
        both = gain * mixed + near_gain * near_mixed
        context[:, lanes] = (both / (gain * total + near_gain * near_total)).astype(BF16)

    sum_copy = pltpu.make_async_remote_copy(
        src_ref=context, dst_ref=context_in, send_sem=sum_send.at[0], recv_sem=sum_recv.at[0],
        device_id=twin, device_id_type=MESH,
    )
    sum_copy.start()
    start = mesh_v[...].astype(F32) - shift + dot(context[...], wo_v[...])
    hidden[...] = start
    start = start.astype(BF16)
    for index, weight in enumerate(processor):
        ahead_sum[index] = dot(start, weight[...])
    sum_copy.wait_recv()

    theirs_in = context_in[...]
    centred = hidden[...] + dot(theirs_in, w_other[...])
    mean = jnp.mean(centred, axis=-1, keepdims=True)
    hidden[...] = centred + shift
    spread = jnp.mean(centred * centred, axis=-1, keepdims=True) - mean * mean
    rise = lax.rsqrt(jnp.maximum(spread, 0.0) + 1e-05)

    raw = [ahead_sum[index] + dot(theirs_in, w_joint[index]) for index in range(3)]

    def projected(index):
        return ((raw[index] - mean * sums[index]) * rise).astype(BF16)

    proc_q, proc_k = projected(0), projected(1)
    probs = []
    for pair in range(pairs):
        lanes = lanes_of(pair)
        logits = dot(two_heads(proc_q[:, lanes]), proc_k[:, lanes], NT) * exponent
        probs.append(jnp.exp2(logits - jnp.max(logits, axis=-1, keepdims=True)).astype(BF16))
    proc_v = projected(2)
    for pair in range(pairs):
        lanes = lanes_of(pair)
        mixed, total = mix(probs[pair], proc_v[:, lanes])
        context_late[:, lanes] = (mixed / total).astype(BF16)

    theirs = pl.ds(pl.multiple_of((1 - core) * own_rows, own_rows), own_rows)
    mine = pl.ds(pl.multiple_of(core * own_rows, own_rows), own_rows)
    last_copy = pltpu.make_async_remote_copy(
        src_ref=context_late.at[theirs], dst_ref=last_in, send_sem=last_sem.at[0],
        recv_sem=last_sem.at[1], device_id=twin, device_id_type=MESH,
    )
    last_copy.start()
    tail[...] = hidden[mine, :] + dot(context_late[mine, :], po_v[...])
    last_copy.wait_recv()
    out[...] = (tail[...] + dot(last_in[...], p_other[...])).astype(BF16)
    for copy in [half_copy, *weight_copies, sum_copy, last_copy]:
        copy.wait_send()
    for slot in range(NEIGH):
        for copy in list_copies(slot):
            copy.wait_send()


def local(*args):
    args = args[:12] + (args[12].T, args[13].T)
    fields, mesh_state = args[0], args[1]
    send_rows = args[11]
    ch, half = fields.shape
    nodes, width = mesh_state.shape
    cols = args[3].shape[1]
    pairs = cols // LANES
    remote = send_rows.shape[1] * send_rows.shape[2]
    columns = 2 * half + remote
    copies = [pltpu.VMEM(x.shape, x.dtype) for x in args]
    buffers = [
        pltpu.VMEM((ch, half), BF16),
        pltpu.VMEM((remote, LANES), BF16),
        pltpu.VMEM((2, remote, LANES), BF16),
        pltpu.VMEM((2 * LANES, 2 * half), BF16),
        pltpu.VMEM((2 * half, LANES), BF16),
        pltpu.VMEM((2 * half, cols), BF16),
        pltpu.VMEM((nodes, columns), F32),
        pltpu.VMEM((pairs * 2 * nodes, 2 * LANES), BF16),
        pltpu.VMEM((nodes, width), F32),
        pltpu.VMEM((nodes, cols), BF16),
        pltpu.VMEM((nodes // 2, width), F32),
        pltpu.VMEM((nodes // 2, cols), BF16),
        pltpu.VMEM((cols, width), BF16),
        pltpu.VMEM((cols, width), BF16),
        pltpu.VMEM((3, cols, cols), BF16),
        pltpu.VMEM((nodes, cols), BF16),
        pltpu.VMEM((3, nodes, cols), F32),
        pltpu.VMEM((nodes, cols), BF16),
    ]
    semaphores = [
        pltpu.SemaphoreType.DMA((len(args),)),
        pltpu.SemaphoreType.DMA((2,)),
        pltpu.SemaphoreType.DMA((2 * NEIGH,)),
        pltpu.SemaphoreType.DMA((2 * NEIGH,)),
        pltpu.SemaphoreType.DMA((2,)),
        pltpu.SemaphoreType.DMA((2,)),
        pltpu.SemaphoreType.DMA((1,)),
        pltpu.SemaphoreType.DMA((1,)),
        pltpu.SemaphoreType.DMA((2,)),
    ] + [pltpu.SemaphoreType.REGULAR] * 2
    return pl.pallas_call(
        kernel,
        out_shape=pltpu.VMEM((nodes // 2, width), BF16),
        in_specs=[pl.BlockSpec(memory_space=pltpu.HBM)] * len(args),
        out_specs=pl.BlockSpec(memory_space=pltpu.VMEM),
        scratch_shapes=copies + buffers + semaphores,
        compiler_params=pltpu.CompilerParams(
            collective_id=0, has_side_effects=True, vmem_limit_bytes=56 * 1024 * 1024
        ),
        cost_estimate=pl.CostEstimate(
            flops=3_000_000_000, bytes_accessed=9_500_000, transcendentals=800_000
        ),
        name="encode_and_process",
    )(*args)


def solution(mesh):
    return jax.shard_map(
        local,
        mesh=mesh,
        in_specs=(
            P(None, ("nodes", "heads")),
            P("nodes", None),
            P(),
            P(None, "heads"),
            P(None, "heads"),
            P(None, "heads"),
            P("heads", None),
            P(None, "heads"),
            P(None, "heads"),
            P(None, "heads"),
            P("heads", None),
            P("nodes", None, None),
            P("nodes", None),
            P("nodes", None),
        ),
        out_specs=P(("nodes", "heads"), None),
        check_vma=False,
    )
```
